512 devices in a mesh: group: 16 (over y, core), dev: 32 (over z, x).
Axes of the slice: x: 4, y: 8, z: 8, core: 2. Of those that a mesh axis runs over, the one named last changes fastest.
Arguments:
- positions: float32 [3, 262144], P(None, ('group', 'dev')), may hold values from -5 to 14, as said below
- strengths: float32 [3, 262144], P(None, ('group', 'dev')), may hold values from -4 to 4
- pair_list: int32 [2, 3072], P(None, ('group', 'dev')), may hold values from 0 to 63, as said below
- pair_count: int32 [512], P(('group', 'dev')), may hold values from 1 to 6, as said below
- far_list: int32 [64, 1024], P(None, ('group', 'dev')), may hold values from 0 to 1023, as said below
Outputs:
- new_positions: float32 [3, 262144], P(None, ('group', 'dev'))
- new_strengths: float32 [3, 262144], P(None, ('group', 'dev'))
The draws below stay inside these ranges and needn't reach their ends.
Inputs may be any that keep to these rules, and one draw needn't show every extreme that they name: `positions`: region g is centred at (3 (g mod 4), 3 ((g div 4) mod 4), 0); every particle lies within 5 of its region's centre in each component. `pair_list`: block numbers within a region; the two blocks of a slot differ. Slots at or beyond the device's count hold arbitrary block numbers of the same range. `pair_count`: some device has all 6 slots live in every draw. `far_list`: every listed cluster lies in another region than the block.
All inputs are finite; a program needn't handle non-finite values.
Results may differ from the reference program's by a relative error of at most 0.0003.
Values sent between devices are 32-bit elements; how exact they have to be, the bound alone decides.
No kernel may reach another device: no remote copies, remote signals or barrier semaphores. Data moves between devices by JAX's collectives and lax.ppermute only.
A program may use at most 64 MiB of HBM per device.

```python
import jax
import jax.numpy as jnp
from jax import lax

BS = 256
NB = 2
MAXP = 6
NFAR = 64
STEPS = 2
BLOCKS = 1024
PARTICLES = 262144
N_GROUP = 16
N_DEV = 32


def draw_positions(key, part):
    key = jax.random.fold_in(key, 5)
    key_block, key_cloud = jax.random.split(key)
    region = jnp.arange(PARTICLES) // (NB * N_DEV * BS)
    centre_x = 3.0 * (region % 4).astype(jnp.float32)
    centre_y = 3.0 * (region // 4 % 4).astype(jnp.float32)
    centre = jnp.stack([centre_x, centre_y, jnp.zeros_like(centre_x)])
    block_shift = jax.random.uniform(key_block, (3, BLOCKS), jnp.float32, -3.0, 3.0)
    scatter = 0.8 * jax.random.normal(key_cloud, (3, PARTICLES), jnp.float32)
    cloud = jnp.repeat(block_shift, BS, axis=1) + scatter
    cloud = jnp.clip(cloud, -5.0, 5.0)
    return (centre + cloud).astype(jnp.float32)


def draw_strengths(key, part):
    key = jax.random.fold_in(key, 47)
    key_common, key_rest = jax.random.split(key)
    common = jax.random.uniform(key_common, (3, BLOCKS), jnp.float32, -1.2, 1.2)
    rest = jnp.clip(jax.random.normal(key_rest, (3, PARTICLES), jnp.float32), -2.5, 2.5)
    values = jnp.repeat(common, BS, axis=1) + rest
    return jnp.clip(values, -4.0, 4.0).astype(jnp.float32)


def draw_pair_list(key, part):
    key = jax.random.fold_in(key, 11)
    key_first, key_offset = jax.random.split(key)
    total_slots = BLOCKS // NB * MAXP
    first = jax.random.randint(key_first, (total_slots,), 0, NB * N_DEV)
    offset = jax.random.randint(key_offset, (total_slots,), 1, NB * N_DEV)
    second = (first + offset) % (NB * N_DEV)
    return jnp.stack([first, second]).astype(jnp.int32)


def draw_pair_count(key, part):
    key = jax.random.fold_in(key, 23)
    key_base, key_heavy, key_where = jax.random.split(key, 3)
    devices_all = BLOCKS // NB
    base = jax.random.randint(key_base, (devices_all,), 1, 4)
    heavy = jax.random.randint(key_heavy, (devices_all,), 0, 8) == 0
    where_full = jax.random.randint(key_where, (), 0, devices_all)
    counts = jnp.where(heavy, MAXP, jnp.minimum(base, MAXP))
    counts = jnp.where(jnp.arange(devices_all) == where_full, MAXP, counts)
    return counts.astype(jnp.int32)


def draw_far_list(key, part):
    key = jax.random.fold_in(key, 37)
    key_region, key_within = jax.random.split(key)
    group_blocks = NB * N_DEV
    region = jnp.arange(BLOCKS) // group_blocks
    other = (region[None, :] + jax.random.randint(key_region, (NFAR, BLOCKS), 1, N_GROUP)) % N_GROUP
    within = jax.random.randint(key_within, (NFAR, BLOCKS), 0, group_blocks)
    return (other * group_blocks + within).astype(jnp.int32)


def setup_inputs(seed: int = 0) -> dict:
    key_of = jax.random.split(jax.random.key(seed), 6)
    return {
        "positions": draw_positions(jax.random.fold_in(key_of[5], 71), 0),
        "strengths": draw_strengths(jax.random.fold_in(key_of[5], 71), 0),
        "pair_list": draw_pair_list(jax.random.fold_in(key_of[5], 71), 0),
        "pair_count": draw_pair_count(jax.random.fold_in(key_of[5], 71), 0),
        "far_list": draw_far_list(jax.random.fold_in(key_of[5], 71), 0),
    }


INV_FOUR_PI = 0.07957747154594767
CORE_SQUARED = 0.25
TIME_STEP = 0.05

def cross_stack(left, right):
    return jnp.stack([left[1] * right[2] - left[2] * right[1], left[2] * right[0] - left[0] * right[2], left[0] * right[1] - left[1] * right[0]])

def one_sided(target_pos, target_str, source_pos, source_str):
    offset = target_pos[:, :, None] - source_pos[:, None, :]
    dist_sq = lax.optimization_barrier(jnp.sum(offset * offset, axis=0)) + CORE_SQUARED
    inv_root = lax.rsqrt(dist_sq)
    first_kernel = inv_root * inv_root * inv_root
    second_kernel = first_kernel * inv_root * inv_root
    source_b = source_str[:, None, :]
    target_a = target_str[:, :, None]
    spin = cross_stack(offset, source_b)
    twist = cross_stack(target_a, source_b)
    align = lax.optimization_barrier(jnp.sum(target_a * offset, axis=0))
    velocity = -INV_FOUR_PI * lax.optimization_barrier(jnp.sum(first_kernel * spin, axis=2))
    stretch = -INV_FOUR_PI * lax.optimization_barrier(jnp.sum(first_kernel * twist - 3.0 * second_kernel * align * spin, axis=2))
    return jnp.concatenate([velocity, stretch], axis=0)

def both_sided(pos_first, str_first, pos_second, str_second):
    offset = pos_first[:, :, None] - pos_second[:, None, :]
    dist_sq = lax.optimization_barrier(jnp.sum(offset * offset, axis=0)) + CORE_SQUARED
    inv_root = lax.rsqrt(dist_sq)
    first_kernel = inv_root * inv_root * inv_root
    second_kernel = first_kernel * inv_root * inv_root
    first_str = str_first[:, :, None]
    second_str = str_second[:, None, :]
    spin_second = cross_stack(offset, second_str)
    spin_first = cross_stack(offset, first_str)
    twist = cross_stack(first_str, second_str)
    align_first = lax.optimization_barrier(jnp.sum(first_str * offset, axis=0))
    align_second = lax.optimization_barrier(jnp.sum(second_str * offset, axis=0))
    vel_first = -INV_FOUR_PI * lax.optimization_barrier(jnp.sum(first_kernel * spin_second, axis=2))
    str_out_first = -INV_FOUR_PI * lax.optimization_barrier(jnp.sum(first_kernel * twist - 3.0 * second_kernel * align_first * spin_second, axis=2))
    vel_second = INV_FOUR_PI * lax.optimization_barrier(jnp.sum(first_kernel * spin_first, axis=1))
    str_out_second = -INV_FOUR_PI * lax.optimization_barrier(jnp.sum(-first_kernel * twist - 3.0 * second_kernel * align_second * spin_first, axis=1))
    return (jnp.concatenate([vel_first, str_out_first], axis=0), jnp.concatenate([vel_second, str_out_second], axis=0))

def reference(positions, strengths, pair_list, pair_count, far_list):
    group_blocks = NB * N_DEV
    for advance in range(STEPS):
        state = jnp.concatenate([positions, strengths], axis=0).reshape(6, BLOCKS, BS)
        centres = lax.optimization_barrier(jnp.mean(state[:3], axis=2))
        totals = lax.optimization_barrier(jnp.sum(state[3:], axis=2))
        moments = jnp.concatenate([centres, totals], axis=0)

        def own_terms(index):
            block = lax.dynamic_index_in_dim(state, index, 1, keepdims=False)
            self_part = one_sided(block[:3], block[3:], block[:3], block[3:])
            far = jnp.take(moments, far_list[:, index], axis=1)
            far_part = one_sided(block[:3], block[3:], far[:3], far[3:])
            return (self_part, far_part)
        self_terms, far_terms = lax.map(own_terms, jnp.arange(BLOCKS, dtype=jnp.int32))

        def visit(accum, slot):
            device = slot // MAXP
            valid = slot % MAXP < pair_count[device]
            base = device // N_DEV * group_blocks
            first = (base + pair_list[0, slot]).astype(jnp.int32)
            second = (base + pair_list[1, slot]).astype(jnp.int32)

            def add(inner):
                block_first = lax.dynamic_index_in_dim(state, first, 1, keepdims=False)
                block_second = lax.dynamic_index_in_dim(state, second, 1, keepdims=False)
                term_first, term_second = both_sided(block_first[:3], block_first[3:], block_second[:3], block_second[3:])
                inner = inner.at[first].add(term_first)
                return inner.at[second].add(term_second)
            return (lax.cond(valid, add, lambda inner: inner, accum), None)
        near_terms = jnp.zeros((BLOCKS, 6, BS), jnp.float32)
        near_terms, unused = lax.scan(visit, near_terms, jnp.arange(BLOCKS // NB * MAXP, dtype=jnp.int32))
        rates = near_terms + self_terms + far_terms
        rates = jnp.transpose(rates, (1, 0, 2)).reshape(6, PARTICLES)
        positions = positions + TIME_STEP * rates[:3]
        strengths = strengths + TIME_STEP * rates[3:]
    return (positions, strengths)
```

```python
import functools

import jax
import jax.numpy as jnp
from jax import lax
from jax.experimental import pallas as pl
from jax.experimental.pallas import tpu as pltpu
from jax.sharding import PartitionSpec as P

BS = 256
STEPS = 2
NZ, NX, NY, NC = 8, 4, 8, 2
N_DEV = NZ * NX
N_GROUP = NY * NC
REGION_BLOCKS = 2 * N_DEV
CHUNK = 32

INV_FOUR_PI = 0.07957747154594767
CORE_SQUARED = 0.25
TIME_STEP = 0.05

VMEM = pltpu.VMEM
SMEM = pltpu.SMEM


def split_rows(rows):
    high = rows.astype(jnp.bfloat16).astype(jnp.float32)
    rest = rows - high
    middle = rest.astype(jnp.bfloat16).astype(jnp.float32)
    parts = [high, middle, rest - middle, jnp.zeros_like(rows)]
    return jnp.concatenate(parts, axis=0).astype(jnp.bfloat16)


def fill_kernels(target, source, mats, count):
    tx, ty, tz = target[0:1], target[1:2], target[2:3]
    ax, ay, az = target[3:4], target[4:5], target[5:6]
    columns = source.T
    for start in range(0, count, CHUNK):
        part = columns[start : start + CHUNK]
        dx = tx - part[:, 0:1]
        dy = ty - part[:, 1:2]
        dz = tz - part[:, 2:3]
        dist_sq = dx * dx + dy * dy + dz * dz + CORE_SQUARED
        inv_root = lax.rsqrt(dist_sq)
        inv_sq = inv_root * inv_root
        first = inv_sq * inv_root
        align = ax * dx + ay * dy + az * dz
        second = first * inv_sq * align
        first_high = first.astype(jnp.bfloat16)
        second_high = second.astype(jnp.bfloat16)
        rows = pl.ds(start, CHUNK)
        mats[0, rows, :] = first_high
        mats[1, rows, :] = (first - first_high.astype(jnp.float32)).astype(jnp.bfloat16)
        mats[2, rows, :] = second_high
        mats[3, rows, :] = (second - second_high.astype(jnp.float32)).astype(jnp.bfloat16)


def weighted_sums(source, mats, count):
    yx, yy, yz = source[0:1], source[1:2], source[2:3]
    bx, by, bz = source[3:4], source[4:5], source[5:6]
    zero = jnp.zeros_like(yx)
    rows = jnp.concatenate(
        [bx, by, bz, yy * bz - yz * by, yz * bx - yx * bz, yx * by - yy * bx, zero, zero], axis=0
    )
    left = split_rows(rows)

    def product(high, low):
        top = jnp.dot(left, mats[high, 0:count, :], preferred_element_type=jnp.float32)
        rest = jnp.dot(left, mats[low, 0:count, :], preferred_element_type=jnp.float32)
        total = top + rest
        return total[0:8] + (total[8:16] + total[16:24])

    return jnp.concatenate([product(0, 1), product(2, 3)], axis=0)


def cross_rows(left, right):
    return jnp.concatenate(
        [
            left[1:2] * right[2:3] - left[2:3] * right[1:2],
            left[2:3] * right[0:1] - left[0:1] * right[2:3],
            left[0:1] * right[1:2] - left[1:2] * right[0:1],
        ],
        axis=0,
    )


def advance_rows(target, sums):
    position, strength = target[0:3], target[3:6]
    velocity = cross_rows(position, sums[0:3]) - sums[3:6]
    twist = cross_rows(strength, sums[0:3])
    spin = cross_rows(position, sums[8:11]) - sums[11:14]
    scale = -INV_FOUR_PI * TIME_STEP
    return scale * jnp.concatenate([velocity, twist - 3.0 * spin], axis=0)


STATE_LANES = 6 * 2 * BS
WIDTH = STATE_LANES + 128


def centre_of(state):
    row = lax.broadcasted_iota(jnp.int32, (8, BS), 0)
    mean = jnp.sum(state, axis=1, keepdims=True) * (1.0 / BS)
    return jnp.where(row < 3, jnp.broadcast_to(mean, (8, BS)), 0.0)


def publish(blocks, info, payload_ref, mine_ref):
    lane = lax.broadcasted_iota(jnp.int32, (8, 128), 1)
    row = lax.broadcasted_iota(jnp.int32, (8, 128), 0)
    table = jnp.zeros((8, 128), jnp.float32)
    for index, block in enumerate(blocks):
        total = jnp.sum(block, axis=1, keepdims=True)
        total = jnp.where(row < 3, total * (1.0 / BS), jnp.broadcast_to(total, (8, 128)))
        table = jnp.where(lane == 8 * index + row, total, table)
        mine_ref[index] = block
    tail = jnp.sum(table, axis=0, keepdims=True)
    if info is not None:
        tail = tail + info
    for device in range(8):
        for c in range(6):
            for index, block in enumerate(blocks):
                payload_ref[device, :, pl.ds(2 * BS * c + BS * index, BS)] = block[c : c + 1]
        payload_ref[device, :, pl.ds(STATE_LANES, 128)] = tail
    for device in range(8, N_DEV, 8):
        payload_ref[device : device + 8] = payload_ref[0:8]


def pack_kernel(pair_ref, count_ref, position_ref, strength_ref, far_ref, row_ref, *out_refs):
    row_ref[...] = jnp.concatenate([far_ref[0:1], far_ref[1:2]], axis=1)
    zero = jnp.zeros((2, 2 * BS), jnp.float32)
    state = jnp.concatenate([position_ref[...], strength_ref[...], zero], axis=0)
    lane = lax.broadcasted_iota(jnp.int32, (1, 128), 1)
    info = jnp.zeros((1, 128), jnp.int32)
    for side in range(2):
        for slot in range(6):
            info = jnp.where(lane == 16 + 6 * side + slot, pair_ref[side, slot], info)
    info = jnp.where(lane == 28, count_ref[0], info)
    publish([state[:, 0:BS], state[:, BS:]], info.astype(jnp.float32), *out_refs)


def visit_counts(base, info):
    lane = lax.broadcasted_iota(jnp.int32, (N_DEV, 128), 1)
    live = info[:, 28:29]
    counts = jnp.zeros((N_DEV, 128), jnp.int32)
    for slot in range(6):
        first = info[:, 16 + slot : 17 + slot]
        second = info[:, 22 + slot : 23 + slot]
        for target, source in ((first, second), (second, first)):
            own = target - base
            code = jnp.where((own >= 0) & (own < 2) & (slot < live), own * 64 + source, -1)
            counts = counts + jnp.where(lane == code, 1, 0)
    return jnp.sum(counts, axis=0, keepdims=True)


def moment_kernel(region_ref, moment_ref):
    columns = region_ref[:, 0, STATE_LANES:].T
    rows = [columns[8 * t + c : 8 * t + c + 1] for c in range(6) for t in range(2)]
    table = jnp.concatenate(rows, axis=1)
    for group in range(N_GROUP):
        moment_ref[group] = table


def self_kernel(mine_ref, *refs):
    if len(refs) == 2:
        out_ref, mats = refs
    else:
        me_ref, region_ref, out_ref, count_ref, mats = refs
        tails = region_ref[:, 0, STATE_LANES:]
        count_ref[...] = visit_counts(2 * me_ref[0], tails.astype(jnp.int32))
    for block in range(2):
        state = mine_ref[block]
        centre = centre_of(state)
        target = state - centre
        fill_kernels(target, target, mats.at[block], BS)
        out_ref[block, 0:16] = weighted_sums(target, mats.at[block], BS)
        out_ref[block, 16:24] = target
        out_ref[block, 24:32] = centre


def visit_list(count_ref, list_ref):
    def add(code, place):
        times = count_ref[0, code]
        list_ref[place] = times * 128 + code
        return place + jnp.where(times > 0, 1, 0)

    place = lax.fori_loop(0, 128, add, jnp.int32(1), unroll=16)
    list_ref[0] = place - 1


def near_kernel(count_ref, self_ref, region_ref, sum_ref, mats, list_ref):
    visit_list(count_ref, list_ref)
    sum_ref[...] = self_ref[:, 0:16]

    def visit(place, slot):
        code = list_ref[place]
        times = (code // 128).astype(jnp.float32)
        block = code // 64 % 2
        source = code % 64
        rows = []
        for c in range(6):
            lanes = pl.ds(pl.multiple_of(2 * BS * c + BS * (source % 2), BS), BS)
            rows.append(region_ref[source // 2, :, lanes])
        rows.append(jnp.zeros((2, BS), jnp.float32))
        rows = jnp.concatenate(rows, axis=0) - self_ref[block, 24:32]
        fill_kernels(self_ref[block, 16:24], rows, mats.at[slot], BS)
        return block, times * weighted_sums(rows, mats.at[slot], BS)

    def visit_two(index, carry):
        block_a, sums_a = visit(2 * index + 1, 0)
        block_b, sums_b = visit(2 * index + 2, 1)
        sum_ref[block_a] += sums_a
        sum_ref[block_b] += sums_b
        return carry

    count = list_ref[0]
    lax.fori_loop(0, count // 2, visit_two, 0)

    @pl.when(count % 2 == 1)
    def _():
        block, sums = visit(count, 0)
        sum_ref[block] += sums


def far_sources(far_ref, moment_ref):
    table = moment_ref[:, 0, :]
    table = jnp.concatenate(
        [table[:, REGION_BLOCKS * c : REGION_BLOCKS * c + REGION_BLOCKS] for c in range(6)], axis=0
    )
    size = table.shape[0]
    high = table.astype(jnp.bfloat16).astype(jnp.float32)
    middle = (table - high).astype(jnp.bfloat16).astype(jnp.float32)
    parts = jnp.concatenate([high, middle, table - high - middle], axis=0).astype(jnp.bfloat16)
    wanted = far_ref[...]
    place = wanted % 2 * N_DEV + wanted % REGION_BLOCKS // 2
    lanes = lax.broadcasted_iota(jnp.int32, (REGION_BLOCKS, 128), 0)
    chosen = jnp.where(lanes == place, 1.0, 0.0).astype(jnp.bfloat16)
    found = jnp.dot(parts, chosen, preferred_element_type=jnp.float32)
    found = found[0:size] + found[size : 2 * size] + found[2 * size :]
    groups = lax.broadcasted_iota(jnp.int32, (N_GROUP, 128), 0)
    mine = groups == wanted // REGION_BLOCKS
    rows = []
    for c in range(6):
        part = found[N_GROUP * c : N_GROUP * c + N_GROUP]
        rows.append(jnp.sum(jnp.where(mine, part, 0.0), axis=0, keepdims=True))
    return jnp.concatenate(rows + [jnp.zeros((2, 128), jnp.float32)], axis=0)


def far_kernel(last, far_ref, mine_ref, self_ref, sum_ref, moment_ref, *refs):
    *outs, mats = refs
    rows = far_sources(far_ref, moment_ref)
    blocks = []
    for block in range(2):
        target = self_ref[block, 16:24]
        source = rows[:, 64 * block : 64 * block + 64] - self_ref[block, 24:32][:, 0:64]
        fill_kernels(target, source, mats.at[block], 64)
        sums = sum_ref[block] + weighted_sums(source, mats.at[block], 64)
        new = mine_ref[block, 0:6] + advance_rows(target, sums)
        blocks.append(jnp.concatenate([new, jnp.zeros((2, BS), jnp.float32)], axis=0))
    if last:
        position_ref, strength_ref = outs
        state = jnp.concatenate(blocks, axis=1)
        position_ref[...] = state[0:3]
        strength_ref[...] = state[3:6]
    else:
        publish(blocks, None, *outs)


def f32(*shape):
    return jax.ShapeDtypeStruct(shape, jnp.float32)


def kept(*shape):
    return pltpu.VMEM(shape, jnp.float32)


def keep(value):
    return pltpu.with_memory_space_constraint(value, VMEM)


def in_vmem(count):
    return [pl.BlockSpec(memory_space=VMEM)] * count


def in_smem(count):
    return [pl.BlockSpec(memory_space=SMEM)] * count


PUBLISHED = (kept(N_DEV, 1, WIDTH), kept(2, 8, BS))


def pack(pair_list, pair_count, positions, strengths, far_list):
    return pl.pallas_call(
        pack_kernel,
        out_shape=(pltpu.VMEM((1, 128), jnp.int32),) + PUBLISHED,
        in_specs=in_smem(2) + in_vmem(3),
        out_specs=tuple(in_vmem(3)),
        name="pack",
    )(pair_list, pair_count, positions, strengths, far_list.T)


def moments_of(region):
    return pl.pallas_call(
        moment_kernel,
        out_shape=kept(N_GROUP, 1, 6 * REGION_BLOCKS),
        in_specs=in_vmem(1),
        out_specs=in_vmem(1)[0],
        name="moments",
    )(region)


def self_terms(mine, *pair_operands):
    out_shape, out_specs, in_specs = (kept(2, 32, BS),), in_vmem(1), in_vmem(1)
    if pair_operands:
        out_shape += (jax.ShapeDtypeStruct((1, 128), jnp.int32),)
        out_specs = in_vmem(2)
        in_specs = in_vmem(1) + in_smem(1) + in_vmem(1)
    return pl.pallas_call(
        self_kernel,
        out_shape=out_shape,
        in_specs=in_specs,
        out_specs=tuple(out_specs),
        scratch_shapes=[pltpu.VMEM((2, 4, BS, BS), jnp.bfloat16)],
        cost_estimate=pl.CostEstimate(flops=4000000, bytes_accessed=60000, transcendentals=130000),
        name="self_terms",
    )(keep(mine), *pair_operands)


def near(counts, own, region):
    return pl.pallas_call(
        near_kernel,
        out_shape=kept(2, 16, BS),
        in_specs=in_smem(1) + in_vmem(2),
        out_specs=in_vmem(1)[0],
        scratch_shapes=[pltpu.VMEM((2, 4, BS, BS), jnp.bfloat16), pltpu.SMEM((136,), jnp.int32)],
        cost_estimate=pl.CostEstimate(flops=20000000, bytes_accessed=600000, transcendentals=500000),
        name="near",
    )(counts, keep(own), region)


def far(far_row, mine, own, sums, moments, last):
    out_shape = (f32(3, 2 * BS), f32(3, 2 * BS)) if last else PUBLISHED
    return pl.pallas_call(
        functools.partial(far_kernel, last),
        out_shape=out_shape,
        in_specs=in_vmem(5),
        out_specs=tuple(in_vmem(len(out_shape))),
        scratch_shapes=[pltpu.VMEM((2, 4, 64, BS), jnp.bfloat16)],
        name="far",
    )(keep(far_row), keep(mine), keep(own), keep(sums), keep(moments))


def exchange(value, axis):
    return lax.all_to_all(value, axis, 0, 0, tiled=True)


def body(positions, strengths, pair_list, pair_count, far_list):
    me = lax.axis_index("dev").astype(jnp.int32).reshape(1)
    far_row, payload, mine = pack(pair_list, pair_count, positions, strengths, far_list)
    counts = None
    for step in range(STEPS):
        first, last = step == 0, step == STEPS - 1
        region = keep(exchange(payload, "dev"))
        moments = exchange(moments_of(region), "group")
        if first:
            own, counts = self_terms(mine, me, region)
        else:
            (own,) = self_terms(mine)
        sums = near(counts, own, region)
        result = far(far_row, mine, own, sums, moments, last)
        if not last:
            payload, mine = result
    return result


def solution(mesh):
    split = P(None, ("group", "dev"))
    return jax.shard_map(
        body,
        mesh=mesh,
        in_specs=(split, split, split, P(("group", "dev")), split),
        out_specs=(split, split),
        check_vma=False,
    )
```

```python
import functools

import jax
import jax.numpy as jnp
from jax import lax
from jax.experimental import pallas as pl
from jax.experimental.pallas import tpu as pltpu
from jax.sharding import PartitionSpec as P

BS = 256
STEPS = 2
NZ, NX, NY, NC = 8, 4, 8, 2
N_DEV = NZ * NX
N_GROUP = NY * NC
REGION_BLOCKS = 2 * N_DEV
CHUNK = 32

INV_FOUR_PI = 0.07957747154594767
CORE_SQUARED = 0.25
TIME_STEP = 0.05

VMEM = pltpu.VMEM
SMEM = pltpu.SMEM


def split_rows(rows):
    high = rows.astype(jnp.bfloat16).astype(jnp.float32)
    rest = rows - high
    middle = rest.astype(jnp.bfloat16).astype(jnp.float32)
    parts = [high, middle, rest - middle, jnp.zeros_like(rows)]
    return jnp.concatenate(parts, axis=0).astype(jnp.bfloat16)


def fill_kernels(target, source, mats, count):
    tx, ty, tz = target[0:1], target[1:2], target[2:3]
    ax, ay, az = target[3:4], target[4:5], target[5:6]
    columns = source.T
    for start in range(0, count, CHUNK):
        part = columns[start : start + CHUNK]
        dx = tx - part[:, 0:1]
        dy = ty - part[:, 1:2]
        dz = tz - part[:, 2:3]
        dist_sq = dx * dx + dy * dy + dz * dz + CORE_SQUARED
        inv_root = lax.rsqrt(dist_sq)
        inv_sq = inv_root * inv_root
        first = inv_sq * inv_root
        align = ax * dx + ay * dy + az * dz
        second = first * inv_sq * align
        first_high = first.astype(jnp.bfloat16)
        second_high = second.astype(jnp.bfloat16)
        rows = pl.ds(start, CHUNK)
        mats[0, rows, :] = first_high
        mats[1, rows, :] = (first - first_high.astype(jnp.float32)).astype(jnp.bfloat16)
        mats[2, rows, :] = second_high
        mats[3, rows, :] = (second - second_high.astype(jnp.float32)).astype(jnp.bfloat16)


def weighted_sums(source, mats, count):
    yx, yy, yz = source[0:1], source[1:2], source[2:3]
    bx, by, bz = source[3:4], source[4:5], source[5:6]
    zero = jnp.zeros_like(yx)
    rows = jnp.concatenate(
        [bx, by, bz, yy * bz - yz * by, yz * bx - yx * bz, yx * by - yy * bx, zero, zero], axis=0
    )
    left = split_rows(rows)

    def product(high, low):
        top = jnp.dot(left, mats[high, 0:count, :], preferred_element_type=jnp.float32)
        rest = jnp.dot(left, mats[low, 0:count, :], preferred_element_type=jnp.float32)
        total = top + rest
        return total[0:8] + (total[8:16] + total[16:24])

    return jnp.concatenate([product(0, 1), product(2, 3)], axis=0)


def cross_rows(left, right):
    return jnp.concatenate(
        [
            left[1:2] * right[2:3] - left[2:3] * right[1:2],
            left[2:3] * right[0:1] - left[0:1] * right[2:3],
            left[0:1] * right[1:2] - left[1:2] * right[0:1],
        ],
        axis=0,
    )


def advance_rows(target, sums):
    position, strength = target[0:3], target[3:6]
    velocity = cross_rows(position, sums[0:3]) - sums[3:6]
    twist = cross_rows(strength, sums[0:3])
    spin = cross_rows(position, sums[8:11]) - sums[11:14]
    scale = -INV_FOUR_PI * TIME_STEP
    return scale * jnp.concatenate([velocity, twist - 3.0 * spin], axis=0)


STATE_LANES = 6 * 2 * BS
WIDTH = STATE_LANES + 128


def centre_of(state):
    row = lax.broadcasted_iota(jnp.int32, (8, BS), 0)
    mean = jnp.sum(state, axis=1, keepdims=True) * (1.0 / BS)
    return jnp.where(row < 3, jnp.broadcast_to(mean, (8, BS)), 0.0)


def publish(blocks, info, payload_ref, mine_ref):
    lane = lax.broadcasted_iota(jnp.int32, (8, 128), 1)
    row = lax.broadcasted_iota(jnp.int32, (8, 128), 0)
    table = jnp.zeros((8, 128), jnp.float32)
    for index, block in enumerate(blocks):
        total = jnp.sum(block, axis=1, keepdims=True)
        total = jnp.where(row < 3, total * (1.0 / BS), jnp.broadcast_to(total, (8, 128)))
        table = jnp.where(lane == 8 * index + row, total, table)
        mine_ref[index] = block
    tail = jnp.sum(table, axis=0, keepdims=True)
    if info is not None:
        tail = tail + info
    for device in range(8):
        for c in range(6):
            for index, block in enumerate(blocks):
                payload_ref[device, :, pl.ds(2 * BS * c + BS * index, BS)] = block[c : c + 1]
        payload_ref[device, :, pl.ds(STATE_LANES, 128)] = tail
    for device in range(8, N_DEV, 8):
        payload_ref[device : device + 8] = payload_ref[0:8]
    if info is not None:
        lane = lax.broadcasted_iota(jnp.int32, (1, 128), 1)
        for device in range(N_DEV):
            payload_ref[device, :, pl.ds(STATE_LANES, 128)] = jnp.where(lane == 29, 1.0 * device, tail)


def pack_kernel(pair_ref, count_ref, position_ref, strength_ref, far_ref, row_ref, *out_refs):
    row_ref[...] = jnp.concatenate([far_ref[0:1], far_ref[1:2]], axis=1)
    zero = jnp.zeros((2, 2 * BS), jnp.float32)
    state = jnp.concatenate([position_ref[...], strength_ref[...], zero], axis=0)
    lane = lax.broadcasted_iota(jnp.int32, (1, 128), 1)
    info = jnp.zeros((1, 128), jnp.int32)
    for side in range(2):
        for slot in range(6):
            info = jnp.where(lane == 16 + 6 * side + slot, pair_ref[side, slot], info)
    info = jnp.where(lane == 28, count_ref[0], info)
    publish([state[:, 0:BS], state[:, BS:]], info.astype(jnp.float32), *out_refs)


def visit_counts(info):
    lane = lax.broadcasted_iota(jnp.int32, (N_DEV, 128), 1)
    first = lane < 22
    partner = jnp.where(first, pltpu.roll(info, 128 - 6, 1), pltpu.roll(info, 6, 1))
    slot = jnp.where(first, lane - 16, lane - 22).astype(jnp.float32)
    own = info - 2.0 * info[:, 29:30]
    live = (slot >= 0.0) & (slot < info[:, 28:29]) & (lane < 28) & (own >= 0.0) & (own < 2.0)
    codes = jnp.where(live, own * 64.0 + partner, -1.0).T
    code = lax.broadcasted_iota(jnp.int32, (128, N_DEV), 0).astype(jnp.float32)
    times = jnp.zeros((128, N_DEV), jnp.float32)
    for row in range(16, 28):
        times = times + jnp.where(code == codes[row : row + 1], 1.0, 0.0)
    counts = lax.dot_general(
        jnp.ones((8, N_DEV), jnp.bfloat16),
        times.astype(jnp.bfloat16),
        (((1,), (1,)), ((), ())),
        preferred_element_type=jnp.float32,
    )
    return counts.astype(jnp.int32)


def moment_kernel(region_ref, moment_ref):
    columns = region_ref[:, 0, STATE_LANES:].T
    rows = [columns[8 * t + c : 8 * t + c + 1] for c in range(6) for t in range(2)]
    table = jnp.concatenate(rows, axis=1)
    for group in range(N_GROUP):
        moment_ref[group] = table


def self_kernel(mine_ref, *refs):
    if len(refs) == 2:
        out_ref, mats = refs
    else:
        region_ref, out_ref, count_ref, mats = refs
        tails = region_ref[:, 0, STATE_LANES:]
        count_ref[...] = visit_counts(tails)
    for block in range(2):
        state = mine_ref[block]
        centre = centre_of(state)
        target = state - centre
        fill_kernels(target, target, mats.at[block], BS)
        out_ref[block, 0:16] = weighted_sums(target, mats.at[block], BS)
        out_ref[block, 16:24] = target
        out_ref[block, 24:32] = centre


def visit_list(count_ref, list_ref):
    def add(code, place):
        times = count_ref[0, code]
        list_ref[place] = times * 128 + code
        return place + jnp.where(times > 0, 1, 0)

    place = lax.fori_loop(0, 128, add, jnp.int32(1), unroll=16)
    list_ref[0] = place - 1


def near_kernel(count_ref, self_ref, region_ref, sum_ref, mats, list_ref, count_smem, sem):
    copy = pltpu.make_async_copy(count_ref, count_smem, sem)
    copy.start()
    copy.wait()
    visit_list(count_smem, list_ref)
    sum_ref[...] = self_ref[:, 0:16]

    def visit(place, slot):
        code = list_ref[place]
        times = (code // 128).astype(jnp.float32)
        block = code // 64 % 2
        source = code % 64
        rows = []
        for c in range(6):
            lanes = pl.ds(pl.multiple_of(2 * BS * c + BS * (source % 2), BS), BS)
            rows.append(region_ref[source // 2, :, lanes])
        rows.append(jnp.zeros((2, BS), jnp.float32))
        rows = jnp.concatenate(rows, axis=0) - self_ref[block, 24:32]
        fill_kernels(self_ref[block, 16:24], rows, mats.at[slot], BS)
        return block, times * weighted_sums(rows, mats.at[slot], BS)

    def visit_two(index, carry):
        block_a, sums_a = visit(2 * index + 1, 0)
        block_b, sums_b = visit(2 * index + 2, 1)
        sum_ref[block_a] += sums_a
        sum_ref[block_b] += sums_b
        return carry

    count = list_ref[0]
    lax.fori_loop(0, count // 2, visit_two, 0)

    @pl.when(count % 2 == 1)
    def _():
        block, sums = visit(count, 0)
        sum_ref[block] += sums


def far_sources(far_ref, moment_ref):
    table = moment_ref[:, 0, :]
    table = jnp.concatenate(
        [table[:, REGION_BLOCKS * c : REGION_BLOCKS * c + REGION_BLOCKS] for c in range(6)], axis=0
    )
    size = table.shape[0]
    high = table.astype(jnp.bfloat16).astype(jnp.float32)
    middle = (table - high).astype(jnp.bfloat16).astype(jnp.float32)
    parts = jnp.concatenate([high, middle, table - high - middle], axis=0).astype(jnp.bfloat16)
    wanted = far_ref[...]
    place = wanted % 2 * N_DEV + wanted % REGION_BLOCKS // 2
    lanes = lax.broadcasted_iota(jnp.int32, (REGION_BLOCKS, 128), 0)
    chosen = jnp.where(lanes == place, 1.0, 0.0).astype(jnp.bfloat16)
    found = jnp.dot(parts, chosen, preferred_element_type=jnp.float32)
    found = found[0:size] + found[size : 2 * size] + found[2 * size :]
    groups = lax.broadcasted_iota(jnp.int32, (N_GROUP, 128), 0)
    mine = groups == wanted // REGION_BLOCKS
    rows = []
    for c in range(6):
        part = found[N_GROUP * c : N_GROUP * c + N_GROUP]
        rows.append(jnp.sum(jnp.where(mine, part, 0.0), axis=0, keepdims=True))
    return jnp.concatenate(rows + [jnp.zeros((2, 128), jnp.float32)], axis=0)


def far_kernel(last, far_ref, mine_ref, self_ref, sum_ref, moment_ref, *refs):
    *outs, mats = refs
    rows = far_sources(far_ref, moment_ref)
    blocks = []
    for block in range(2):
        target = self_ref[block, 16:24]
        source = rows[:, 64 * block : 64 * block + 64] - self_ref[block, 24:32][:, 0:64]
        fill_kernels(target, source, mats.at[block], 64)
        sums = sum_ref[block] + weighted_sums(source, mats.at[block], 64)
        new = mine_ref[block, 0:6] + advance_rows(target, sums)
        blocks.append(jnp.concatenate([new, jnp.zeros((2, BS), jnp.float32)], axis=0))
    if last:
        position_ref, strength_ref = outs
        state = jnp.concatenate(blocks, axis=1)
        position_ref[...] = state[0:3]
        strength_ref[...] = state[3:6]
    else:
        publish(blocks, None, *outs)


def f32(*shape):
    return jax.ShapeDtypeStruct(shape, jnp.float32)


def kept(*shape):
    return pltpu.VMEM(shape, jnp.float32)


def keep(value):
    return pltpu.with_memory_space_constraint(value, VMEM)


def in_vmem(count):
    return [pl.BlockSpec(memory_space=VMEM)] * count


def in_smem(count):
    return [pl.BlockSpec(memory_space=SMEM)] * count


PUBLISHED = (kept(N_DEV, 1, WIDTH), kept(2, 8, BS))


def pack(pair_list, pair_count, positions, strengths, far_list):
    return pl.pallas_call(
        pack_kernel,
        out_shape=(pltpu.VMEM((1, 128), jnp.int32),) + PUBLISHED,
        in_specs=in_smem(2) + in_vmem(3),
        out_specs=tuple(in_vmem(3)),
        name="pack",
    )(pair_list, pair_count, positions, strengths, far_list.T)


def moments_of(region):
    return pl.pallas_call(
        moment_kernel,
        out_shape=kept(N_GROUP, 1, 6 * REGION_BLOCKS),
        in_specs=in_vmem(1),
        out_specs=in_vmem(1)[0],
        name="moments",
    )(region)


def self_terms(mine, *pair_operands):
    out_shape, out_specs, in_specs = (kept(2, 32, BS),), in_vmem(1), in_vmem(1)
    if pair_operands:
        out_shape += (pltpu.VMEM((8, 128), jnp.int32),)
        out_specs = in_vmem(2)
        in_specs = in_vmem(2)
    return pl.pallas_call(
        self_kernel,
        out_shape=out_shape,
        in_specs=in_specs,
        out_specs=tuple(out_specs),
        scratch_shapes=[pltpu.VMEM((2, 4, BS, BS), jnp.bfloat16)],
        cost_estimate=pl.CostEstimate(flops=4000000, bytes_accessed=60000, transcendentals=130000),
        name="self_terms",
    )(keep(mine), *pair_operands)


def near(counts, own, region):
    return pl.pallas_call(
        near_kernel,
        out_shape=kept(2, 16, BS),
        in_specs=in_vmem(3),
        out_specs=in_vmem(1)[0],
        scratch_shapes=[
            pltpu.VMEM((2, 4, BS, BS), jnp.bfloat16),
            pltpu.SMEM((136,), jnp.int32),
            pltpu.SMEM((8, 128), jnp.int32),
            pltpu.SemaphoreType.DMA(()),
        ],
        cost_estimate=pl.CostEstimate(flops=20000000, bytes_accessed=600000, transcendentals=500000),
        name="near",
    )(keep(counts), keep(own), region)


def far(far_row, mine, own, sums, moments, last):
    out_shape = (f32(3, 2 * BS), f32(3, 2 * BS)) if last else PUBLISHED
    return pl.pallas_call(
        functools.partial(far_kernel, last),
        out_shape=out_shape,
        in_specs=in_vmem(5),
        out_specs=tuple(in_vmem(len(out_shape))),
        scratch_shapes=[pltpu.VMEM((2, 4, 64, BS), jnp.bfloat16)],
        name="far",
    )(keep(far_row), keep(mine), keep(own), keep(sums), keep(moments))


def exchange(value, axis):
    return lax.all_to_all(value, axis, 0, 0, tiled=True)


def body(positions, strengths, pair_list, pair_count, far_list):
    far_row, payload, mine = pack(pair_list, pair_count, positions, strengths, far_list)
    counts = None
    for step in range(STEPS):
        first, last = step == 0, step == STEPS - 1
        region = keep(exchange(payload, "dev"))
        moments = exchange(moments_of(region), "group")
        if first:
            own, counts = self_terms(mine, region)
        else:
            (own,) = self_terms(mine)
        sums = near(counts, own, region)
        result = far(far_row, mine, own, sums, moments, last)
        if not last:
            payload, mine = result
    return result


def solution(mesh):
    split = P(None, ("group", "dev"))
    return jax.shard_map(
        body,
        mesh=mesh,
        in_specs=(split, split, split, P(("group", "dev")), split),
        out_specs=(split, split),
        check_vma=False,
    )
```

```python
import functools

import jax
import jax.numpy as jnp
from jax import lax
from jax.experimental import pallas as pl
from jax.experimental.pallas import tpu as pltpu
from jax.sharding import PartitionSpec as P

BS = 256
STEPS = 2
NZ, NX, NY, NC = 8, 4, 8, 2
N_DEV = NZ * NX
N_GROUP = NY * NC
REGION_BLOCKS = 2 * N_DEV
CHUNK = 32

INV_FOUR_PI = 0.07957747154594767
CORE_SQUARED = 0.25
TIME_STEP = 0.05

VMEM = pltpu.VMEM
SMEM = pltpu.SMEM


def split_rows(rows):
    high = rows.astype(jnp.bfloat16).astype(jnp.float32)
    rest = rows - high
    middle = rest.astype(jnp.bfloat16).astype(jnp.float32)
    parts = [high, middle, rest - middle, jnp.zeros_like(rows)]
    return jnp.concatenate(parts, axis=0).astype(jnp.bfloat16)


def fill_kernels(target, source, mats, count):
    tx, ty, tz = target[0:1], target[1:2], target[2:3]
    ax, ay, az = target[3:4], target[4:5], target[5:6]
    columns = source.T
    for start in range(0, count, CHUNK):
        part = columns[start : start + CHUNK]
        dx = tx - part[:, 0:1]
        dy = ty - part[:, 1:2]
        dz = tz - part[:, 2:3]
        dist_sq = dx * dx + dy * dy + dz * dz + CORE_SQUARED
        inv_root = lax.rsqrt(dist_sq)
        inv_sq = inv_root * inv_root
        first = inv_sq * inv_root
        align = ax * dx + ay * dy + az * dz
        second = first * inv_sq * align
        first_high = first.astype(jnp.bfloat16)
        second_high = second.astype(jnp.bfloat16)
        rows = pl.ds(start, CHUNK)
        mats[0, rows, :] = first_high
        mats[1, rows, :] = (first - first_high.astype(jnp.float32)).astype(jnp.bfloat16)
        mats[2, rows, :] = second_high
        mats[3, rows, :] = (second - second_high.astype(jnp.float32)).astype(jnp.bfloat16)


def weighted_sums(source, mats, count):
    yx, yy, yz = source[0:1], source[1:2], source[2:3]
    bx, by, bz = source[3:4], source[4:5], source[5:6]
    zero = jnp.zeros_like(yx)
    rows = jnp.concatenate(
        [bx, by, bz, yy * bz - yz * by, yz * bx - yx * bz, yx * by - yy * bx, zero, zero], axis=0
    )
    left = split_rows(rows)

    def product(high, low):
        top = jnp.dot(left, mats[high, 0:count, :], preferred_element_type=jnp.float32)
        rest = jnp.dot(left, mats[low, 0:count, :], preferred_element_type=jnp.float32)
        total = top + rest
        return total[0:8] + (total[8:16] + total[16:24])

    return jnp.concatenate([product(0, 1), product(2, 3)], axis=0)


def cross_rows(left, right):
    return jnp.concatenate(
        [
            left[1:2] * right[2:3] - left[2:3] * right[1:2],
            left[2:3] * right[0:1] - left[0:1] * right[2:3],
            left[0:1] * right[1:2] - left[1:2] * right[0:1],
        ],
        axis=0,
    )


def advance_rows(target, sums):
    position, strength = target[0:3], target[3:6]
    velocity = cross_rows(position, sums[0:3]) - sums[3:6]
    twist = cross_rows(strength, sums[0:3])
    spin = cross_rows(position, sums[8:11]) - sums[11:14]
    scale = -INV_FOUR_PI * TIME_STEP
    return scale * jnp.concatenate([velocity, twist - 3.0 * spin], axis=0)


STATE_LANES = 6 * 2 * BS
WIDTH = STATE_LANES + 128


def centre_of(state):
    row = lax.broadcasted_iota(jnp.int32, (8, BS), 0)
    mean = jnp.sum(state, axis=1, keepdims=True) * (1.0 / BS)
    return jnp.where(row < 3, jnp.broadcast_to(mean, (8, BS)), 0.0)


def publish(blocks, info, payload_ref, mine_ref):
    lane = lax.broadcasted_iota(jnp.int32, (8, 128), 1)
    row = lax.broadcasted_iota(jnp.int32, (8, 128), 0)
    table = jnp.zeros((8, 128), jnp.float32)
    for index, block in enumerate(blocks):
        total = jnp.sum(block, axis=1, keepdims=True)
        total = jnp.where(row < 3, total * (1.0 / BS), jnp.broadcast_to(total, (8, 128)))
        table = jnp.where(lane == 8 * index + row, total, table)
        mine_ref[index] = block
    tail = jnp.sum(table, axis=0, keepdims=True)
    if info is not None:
        tail = tail + info
    for device in range(8):
        for c in range(6):
            for index, block in enumerate(blocks):
                payload_ref[device, :, pl.ds(2 * BS * c + BS * index, BS)] = block[c : c + 1]
        payload_ref[device, :, pl.ds(STATE_LANES, 128)] = tail
    for device in range(8, N_DEV, 8):
        payload_ref[device : device + 8] = payload_ref[0:8]
    if info is not None:
        lane = lax.broadcasted_iota(jnp.int32, (1, 128), 1)
        for device in range(N_DEV):
            payload_ref[device, :, pl.ds(STATE_LANES, 128)] = jnp.where(lane == 29, 1.0 * device, tail)


def pack_kernel(pair_ref, count_ref, position_ref, strength_ref, far_ref, row_ref, *out_refs):
    row_ref[...] = jnp.concatenate([far_ref[0:1], far_ref[1:2]], axis=1)
    zero = jnp.zeros((2, 2 * BS), jnp.float32)
    state = jnp.concatenate([position_ref[...], strength_ref[...], zero], axis=0)
    lane = lax.broadcasted_iota(jnp.int32, (1, 128), 1)
    info = jnp.zeros((1, 128), jnp.int32)
    for side in range(2):
        for slot in range(6):
            info = jnp.where(lane == 16 + 6 * side + slot, pair_ref[side, slot], info)
    info = jnp.where(lane == 28, count_ref[0], info)
    publish([state[:, 0:BS], state[:, BS:]], info.astype(jnp.float32), *out_refs)


def visit_counts(info):
    lane = lax.broadcasted_iota(jnp.int32, (N_DEV, 128), 1)
    first = lane < 22
    partner = jnp.where(first, pltpu.roll(info, 128 - 6, 1), pltpu.roll(info, 6, 1))
    slot = jnp.where(first, lane - 16, lane - 22).astype(jnp.float32)
    own = info - 2.0 * info[:, 29:30]
    live = (slot >= 0.0) & (slot < info[:, 28:29]) & (lane < 28) & (own >= 0.0) & (own < 2.0)
    codes = jnp.where(live, own * 64.0 + partner, -1.0).T
    code = lax.broadcasted_iota(jnp.int32, (128, N_DEV), 0).astype(jnp.float32)
    times = jnp.zeros((128, N_DEV), jnp.float32)
    for row in range(16, 28):
        times = times + jnp.where(code == codes[row : row + 1], 1.0, 0.0)
    counts = lax.dot_general(
        jnp.ones((8, N_DEV), jnp.float32),
        times,
        (((1,), (1,)), ((), ())),
        preferred_element_type=jnp.float32,
    )
    return counts.astype(jnp.int32)


def moment_kernel(region_ref, moment_ref):
    columns = region_ref[:, 0, STATE_LANES:].T
    rows = [columns[8 * t + c : 8 * t + c + 1] for c in range(6) for t in range(2)]
    table = jnp.concatenate(rows, axis=1)
    for group in range(N_GROUP):
        moment_ref[group] = table


def self_kernel(mine_ref, *refs):
    if len(refs) == 2:
        out_ref, mats = refs
    else:
        region_ref, out_ref, count_ref, mats = refs
        tails = region_ref[:, 0, STATE_LANES:]
        count_ref[...] = visit_counts(tails)
    for block in range(2):
        state = mine_ref[block]
        centre = centre_of(state)
        target = state - centre
        fill_kernels(target, target, mats.at[block], BS)
        out_ref[block, 0:16] = weighted_sums(target, mats.at[block], BS)
        out_ref[block, 16:24] = target
        out_ref[block, 24:32] = centre


def visit_list(count_ref, list_ref):
    def add(code, place):
        times = count_ref[0, code]
        list_ref[place] = times * 128 + code
        return place + jnp.where(times > 0, 1, 0)

    place = lax.fori_loop(0, 128, add, jnp.int32(1), unroll=16)
    list_ref[0] = place - 1


def near_kernel(count_ref, self_ref, region_ref, sum_ref, mats, list_ref, count_smem, sem):
    copy = pltpu.make_async_copy(count_ref, count_smem, sem)
    copy.start()
    copy.wait()
    visit_list(count_smem, list_ref)
    sum_ref[...] = self_ref[:, 0:16]

    def visit(place, slot):
        code = list_ref[place]
        times = (code >> 7).astype(jnp.float32)
        block = (code >> 6) & 1
        source = code & 63
        rows = []
        for c in range(6):
            lanes = pl.ds(pl.multiple_of(2 * BS * c + BS * (source & 1), BS), BS)
            rows.append(region_ref[source >> 1, :, lanes])
        rows.append(jnp.zeros((2, BS), jnp.float32))
        rows = jnp.concatenate(rows, axis=0) - self_ref[block, 24:32]
        fill_kernels(self_ref[block, 16:24], rows, mats.at[slot], BS)
        return block, times * weighted_sums(rows, mats.at[slot], BS)

    def visit_two(index, carry):
        block_a, sums_a = visit(2 * index + 1, 0)
        block_b, sums_b = visit(2 * index + 2, 1)
        sum_ref[block_a] += sums_a
        sum_ref[block_b] += sums_b
        return carry

    count = list_ref[0]
    lax.fori_loop(0, count >> 1, visit_two, 0)

    @pl.when(count & 1 == 1)
    def _():
        block, sums = visit(count, 0)
        sum_ref[block] += sums


def far_sources(far_ref, moment_ref):
    table = moment_ref[:, 0, :]
    table = jnp.concatenate(
        [table[:, REGION_BLOCKS * c : REGION_BLOCKS * c + REGION_BLOCKS] for c in range(6)], axis=0
    )
    size = table.shape[0]
    high = table.astype(jnp.bfloat16).astype(jnp.float32)
    middle = (table - high).astype(jnp.bfloat16).astype(jnp.float32)
    parts = jnp.concatenate([high, middle, table - high - middle], axis=0).astype(jnp.bfloat16)
    wanted = far_ref[...]
    place = (wanted & 1) * N_DEV + ((wanted >> 1) & (N_DEV - 1))
    lanes = lax.broadcasted_iota(jnp.int32, (REGION_BLOCKS, 128), 0)
    chosen = jnp.where(lanes == place, 1.0, 0.0).astype(jnp.bfloat16)
    found = jnp.dot(parts, chosen, preferred_element_type=jnp.float32)
    found = found[0:size] + found[size : 2 * size] + found[2 * size :]
    groups = lax.broadcasted_iota(jnp.int32, (N_GROUP, 128), 0)
    mine = groups == wanted >> 6
    rows = []
    for c in range(6):
        part = found[N_GROUP * c : N_GROUP * c + N_GROUP]
        rows.append(jnp.sum(jnp.where(mine, part, 0.0), axis=0, keepdims=True))
    return jnp.concatenate(rows + [jnp.zeros((2, 128), jnp.float32)], axis=0)


def far_kernel(last, far_ref, mine_ref, self_ref, sum_ref, moment_ref, *refs):
    *outs, mats = refs
    rows = far_sources(far_ref, moment_ref)
    blocks = []
    for block in range(2):
        target = self_ref[block, 16:24]
        source = rows[:, 64 * block : 64 * block + 64] - self_ref[block, 24:32][:, 0:64]
        fill_kernels(target, source, mats.at[block], 64)
        sums = sum_ref[block] + weighted_sums(source, mats.at[block], 64)
        new = mine_ref[block, 0:6] + advance_rows(target, sums)
        blocks.append(jnp.concatenate([new, jnp.zeros((2, BS), jnp.float32)], axis=0))
    if last:
        position_ref, strength_ref = outs
        state = jnp.concatenate(blocks, axis=1)
        position_ref[...] = state[0:3]
        strength_ref[...] = state[3:6]
    else:
        publish(blocks, None, *outs)


def f32(*shape):
    return jax.ShapeDtypeStruct(shape, jnp.float32)


def kept(*shape):
    return pltpu.VMEM(shape, jnp.float32)


def keep(value):
    return pltpu.with_memory_space_constraint(value, VMEM)


def in_vmem(count):
    return [pl.BlockSpec(memory_space=VMEM)] * count


def in_smem(count):
    return [pl.BlockSpec(memory_space=SMEM)] * count


PUBLISHED = (kept(N_DEV, 1, WIDTH), kept(2, 8, BS))


def pack(pair_list, pair_count, positions, strengths, far_list):
    return pl.pallas_call(
        pack_kernel,
        out_shape=(pltpu.VMEM((1, 128), jnp.int32),) + PUBLISHED,
        in_specs=in_smem(2) + in_vmem(3),
        out_specs=tuple(in_vmem(3)),
        name="pack",
    )(pair_list, pair_count, positions, strengths, far_list.T)


def moments_of(region):
    return pl.pallas_call(
        moment_kernel,
        out_shape=kept(N_GROUP, 1, 6 * REGION_BLOCKS),
        in_specs=in_vmem(1),
        out_specs=in_vmem(1)[0],
        name="moments",
    )(region)


def self_terms(mine, *pair_operands):
    out_shape, out_specs, in_specs = (kept(2, 32, BS),), in_vmem(1), in_vmem(1)
    if pair_operands:
        out_shape += (pltpu.VMEM((8, 128), jnp.int32),)
        out_specs = in_vmem(2)
        in_specs = in_vmem(2)
    return pl.pallas_call(
        self_kernel,
        out_shape=out_shape,
        in_specs=in_specs,
        out_specs=tuple(out_specs),
        scratch_shapes=[pltpu.VMEM((2, 4, BS, BS), jnp.bfloat16)],
        cost_estimate=pl.CostEstimate(flops=4000000, bytes_accessed=60000, transcendentals=130000),
        name="self_terms",
    )(keep(mine), *pair_operands)


def near(counts, own, region):
    return pl.pallas_call(
        near_kernel,
        out_shape=kept(2, 16, BS),
        in_specs=in_vmem(3),
        out_specs=in_vmem(1)[0],
        scratch_shapes=[
            pltpu.VMEM((2, 4, BS, BS), jnp.bfloat16),
            pltpu.SMEM((136,), jnp.int32),
            pltpu.SMEM((8, 128), jnp.int32),
            pltpu.SemaphoreType.DMA(()),
        ],
        cost_estimate=pl.CostEstimate(flops=20000000, bytes_accessed=600000, transcendentals=500000),
        name="near",
    )(keep(counts), keep(own), region)


def far(far_row, mine, own, sums, moments, last):
    out_shape = (f32(3, 2 * BS), f32(3, 2 * BS)) if last else PUBLISHED
    return pl.pallas_call(
        functools.partial(far_kernel, last),
        out_shape=out_shape,
        in_specs=in_vmem(5),
        out_specs=tuple(in_vmem(len(out_shape))),
        scratch_shapes=[pltpu.VMEM((2, 4, 64, BS), jnp.bfloat16)],
        name="far",
    )(keep(far_row), keep(mine), keep(own), keep(sums), keep(moments))


def exchange(value, axis):
    return lax.all_to_all(value, axis, 0, 0, tiled=True)


def body(positions, strengths, pair_list, pair_count, far_list):
    far_row, payload, mine = pack(pair_list, pair_count, positions, strengths, far_list)
    counts = None
    for step in range(STEPS):
        first, last = step == 0, step == STEPS - 1
        region = keep(exchange(payload, "dev"))
        moments = exchange(moments_of(region), "group")
        if first:
            own, counts = self_terms(mine, region)
        else:
            (own,) = self_terms(mine)
        sums = near(counts, own, region)
        result = far(far_row, mine, own, sums, moments, last)
        if not last:
            payload, mine = result
    return result


def solution(mesh):
    split = P(None, ("group", "dev"))
    return jax.shard_map(
        body,
        mesh=mesh,
        in_specs=(split, split, split, P(("group", "dev")), split),
        out_specs=(split, split),
        check_vma=False,
    )
```

```python
import functools

import jax
import jax.numpy as jnp
from jax import lax
from jax.experimental import pallas as pl
from jax.experimental.pallas import tpu as pltpu
from jax.sharding import PartitionSpec as P

BS = 256
STEPS = 2
NZ, NX, NY, NC = 8, 4, 8, 2
N_DEV = NZ * NX
N_GROUP = NY * NC
REGION_BLOCKS = 2 * N_DEV
CHUNK = 32

INV_FOUR_PI = 0.07957747154594767
CORE_SQUARED = 0.25
TIME_STEP = 0.05

VMEM = pltpu.VMEM
SMEM = pltpu.SMEM


def split_rows(rows):
    high = rows.astype(jnp.bfloat16).astype(jnp.float32)
    rest = rows - high
    middle = rest.astype(jnp.bfloat16).astype(jnp.float32)
    parts = [high, middle, rest - middle, jnp.zeros_like(rows)]
    return jnp.concatenate(parts, axis=0).astype(jnp.bfloat16)


def fill_kernels(target, source, mats, count):
    tx, ty, tz = target[0:1], target[1:2], target[2:3]
    ax, ay, az = target[3:4], target[4:5], target[5:6]
    columns = source.T
    for start in range(0, count, CHUNK):
        part = columns[start : start + CHUNK]
        dx = tx - part[:, 0:1]
        dy = ty - part[:, 1:2]
        dz = tz - part[:, 2:3]
        dist_sq = dx * dx + dy * dy + dz * dz + CORE_SQUARED
        inv_root = lax.rsqrt(dist_sq)
        inv_sq = inv_root * inv_root
        first = inv_sq * inv_root
        align = ax * dx + ay * dy + az * dz
        second = first * inv_sq * align
        first_high = first.astype(jnp.bfloat16)
        second_high = second.astype(jnp.bfloat16)
        rows = pl.ds(start, CHUNK)
        mats[0, rows, :] = first_high
        mats[1, rows, :] = (first - first_high.astype(jnp.float32)).astype(jnp.bfloat16)
        mats[2, rows, :] = second_high
        mats[3, rows, :] = (second - second_high.astype(jnp.float32)).astype(jnp.bfloat16)


def weighted_sums(source, mats, count):
    yx, yy, yz = source[0:1], source[1:2], source[2:3]
    bx, by, bz = source[3:4], source[4:5], source[5:6]
    zero = jnp.zeros_like(yx)
    rows = jnp.concatenate(
        [bx, by, bz, yy * bz - yz * by, yz * bx - yx * bz, yx * by - yy * bx, zero, zero], axis=0
    )
    left = split_rows(rows)

    def product(high, low):
        top = jnp.dot(left, mats[high, 0:count, :], preferred_element_type=jnp.float32)
        rest = jnp.dot(left, mats[low, 0:count, :], preferred_element_type=jnp.float32)
        total = top + rest
        return total[0:8] + (total[8:16] + total[16:24])

    return jnp.concatenate([product(0, 1), product(2, 3)], axis=0)


def cross_rows(left, right):
    return jnp.concatenate(
        [
            left[1:2] * right[2:3] - left[2:3] * right[1:2],
            left[2:3] * right[0:1] - left[0:1] * right[2:3],
            left[0:1] * right[1:2] - left[1:2] * right[0:1],
        ],
        axis=0,
    )


def advance_rows(target, sums):
    position, strength = target[0:3], target[3:6]
    velocity = cross_rows(position, sums[0:3]) - sums[3:6]
    twist = cross_rows(strength, sums[0:3])
    spin = cross_rows(position, sums[8:11]) - sums[11:14]
    scale = -INV_FOUR_PI * TIME_STEP
    return scale * jnp.concatenate([velocity, twist - 3.0 * spin], axis=0)


STATE_LANES = 6 * 2 * BS
WIDTH = STATE_LANES + 128


def centre_of(state):
    row = lax.broadcasted_iota(jnp.int32, (8, BS), 0)
    mean = jnp.sum(state, axis=1, keepdims=True) * (1.0 / BS)
    return jnp.where(row < 3, jnp.broadcast_to(mean, (8, BS)), 0.0)


def publish(blocks, info, payload_ref, mine_ref):
    lane = lax.broadcasted_iota(jnp.int32, (8, 128), 1)
    row = lax.broadcasted_iota(jnp.int32, (8, 128), 0)
    table = jnp.zeros((8, 128), jnp.float32)
    for index, block in enumerate(blocks):
        total = jnp.sum(block, axis=1, keepdims=True)
        total = jnp.where(row < 3, total * (1.0 / BS), jnp.broadcast_to(total, (8, 128)))
        table = jnp.where(lane == 8 * index + row, total, table)
        mine_ref[index] = block
    tail = jnp.sum(table, axis=0, keepdims=True)
    if info is not None:
        tail = tail + info
    for device in range(8):
        for c in range(6):
            for index, block in enumerate(blocks):
                payload_ref[device, :, pl.ds(2 * BS * c + BS * index, BS)] = block[c : c + 1]
        payload_ref[device, :, pl.ds(STATE_LANES, 128)] = tail
    for device in range(8, N_DEV, 8):
        payload_ref[device : device + 8] = payload_ref[0:8]
    if info is not None:
        lane = lax.broadcasted_iota(jnp.int32, (1, 128), 1)
        for device in range(N_DEV):
            payload_ref[device, :, pl.ds(STATE_LANES, 128)] = jnp.where(lane == 29, 1.0 * device, tail)


def pack_kernel(pair_ref, count_ref, position_ref, strength_ref, far_ref, row_ref, *out_refs):
    row_ref[...] = jnp.concatenate([far_ref[0:1], far_ref[1:2]], axis=1)
    zero = jnp.zeros((2, 2 * BS), jnp.float32)
    state = jnp.concatenate([position_ref[...], strength_ref[...], zero], axis=0)
    lane = lax.broadcasted_iota(jnp.int32, (1, 128), 1)
    info = jnp.zeros((1, 128), jnp.int32)
    for side in range(2):
        for slot in range(6):
            info = jnp.where(lane == 16 + 6 * side + slot, pair_ref[side, slot], info)
    info = jnp.where(lane == 28, count_ref[0], info)
    publish([state[:, 0:BS], state[:, BS:]], info.astype(jnp.float32), *out_refs)


def visit_counts(info):
    lane = lax.broadcasted_iota(jnp.int32, (N_DEV, 128), 1)
    first = lane < 22
    partner = jnp.where(first, pltpu.roll(info, 128 - 6, 1), pltpu.roll(info, 6, 1))
    slot = jnp.where(first, lane - 16, lane - 22).astype(jnp.float32)
    own = info - 2.0 * info[:, 29:30]
    live = (slot >= 0.0) & (slot < info[:, 28:29]) & (lane < 28) & (own >= 0.0) & (own < 2.0)
    codes = jnp.where(live, own * 64.0 + partner, -1.0).T
    code = lax.broadcasted_iota(jnp.int32, (128, N_DEV), 0).astype(jnp.float32)
    times = jnp.zeros((128, N_DEV), jnp.float32)
    for row in range(16, 28):
        times = times + jnp.where(code == codes[row : row + 1], 1.0, 0.0)
    counts = lax.dot_general(
        jnp.ones((8, N_DEV), jnp.float32),
        times,
        (((1,), (1,)), ((), ())),
        preferred_element_type=jnp.float32,
    )
    return counts.astype(jnp.int32)


def moment_kernel(region_ref, moment_ref):
    columns = region_ref[:, 0, STATE_LANES:].T
    rows = [columns[8 * t + c : 8 * t + c + 1] for c in range(6) for t in range(2)]
    table = jnp.concatenate(rows, axis=1)
    for group in range(N_GROUP):
        moment_ref[group] = table


def own_terms(blocks, out_ref, mats):
    for block, state in enumerate(blocks):
        centre = centre_of(state)
        target = state - centre
        fill_kernels(target, target, mats.at[block], BS)
        out_ref[block, 0:16] = weighted_sums(target, mats.at[block], BS)
        out_ref[block, 16:24] = target
        out_ref[block, 24:32] = centre


def first_self_kernel(mine_ref, region_ref, out_ref, count_ref, mats):
    count_ref[...] = visit_counts(region_ref[:, 0, STATE_LANES:])
    own_terms([mine_ref[0], mine_ref[1]], out_ref, mats)


def later_self_kernel(core_ref, mine_ref, early_ref, out_ref, mats):
    @pl.when(core_ref[0] == 0)
    def _():
        own_terms([mine_ref[0], mine_ref[1]], out_ref, mats)

    @pl.when(core_ref[0] != 0)
    def _():
        out_ref[...] = early_ref[...]


def visit_list(count_ref, list_ref):
    def add(code, place):
        times = count_ref[0, code]
        list_ref[place] = times * 128 + code
        return place + jnp.where(times > 0, 1, 0)

    place = lax.fori_loop(0, 128, add, jnp.int32(1), unroll=16)
    list_ref[0] = place - 1


def near_kernel(count_ref, self_ref, region_ref, sum_ref, mats, list_ref, count_smem, sem):
    copy = pltpu.make_async_copy(count_ref, count_smem, sem)
    copy.start()
    copy.wait()
    visit_list(count_smem, list_ref)
    sum_ref[...] = self_ref[:, 0:16]

    def visit(place, slot):
        code = list_ref[place]
        times = (code >> 7).astype(jnp.float32)
        block = (code >> 6) & 1
        source = code & 63
        rows = []
        for c in range(6):
            lanes = pl.ds(pl.multiple_of(2 * BS * c + BS * (source & 1), BS), BS)
            rows.append(region_ref[source >> 1, :, lanes])
        rows.append(jnp.zeros((2, BS), jnp.float32))
        rows = jnp.concatenate(rows, axis=0) - self_ref[block, 24:32]
        fill_kernels(self_ref[block, 16:24], rows, mats.at[slot], BS)
        return block, times * weighted_sums(rows, mats.at[slot], BS)

    def visit_two(index, carry):
        block_a, sums_a = visit(2 * index + 1, 0)
        block_b, sums_b = visit(2 * index + 2, 1)
        sum_ref[block_a] += sums_a
        sum_ref[block_b] += sums_b
        return carry

    count = list_ref[0]
    lax.fori_loop(0, count >> 1, visit_two, 0)

    @pl.when(count & 1 == 1)
    def _():
        block, sums = visit(count, 0)
        sum_ref[block] += sums


def far_sources(far_ref, moment_ref):
    table = moment_ref[:, 0, :]
    table = jnp.concatenate(
        [table[:, REGION_BLOCKS * c : REGION_BLOCKS * c + REGION_BLOCKS] for c in range(6)], axis=0
    )
    size = table.shape[0]
    high = table.astype(jnp.bfloat16).astype(jnp.float32)
    middle = (table - high).astype(jnp.bfloat16).astype(jnp.float32)
    parts = jnp.concatenate([high, middle, table - high - middle], axis=0).astype(jnp.bfloat16)
    wanted = far_ref[...]
    place = (wanted & 1) * N_DEV + ((wanted >> 1) & (N_DEV - 1))
    lanes = lax.broadcasted_iota(jnp.int32, (REGION_BLOCKS, 128), 0)
    chosen = jnp.where(lanes == place, 1.0, 0.0).astype(jnp.bfloat16)
    found = jnp.dot(parts, chosen, preferred_element_type=jnp.float32)
    found = found[0:size] + found[size : 2 * size] + found[2 * size :]
    groups = lax.broadcasted_iota(jnp.int32, (N_GROUP, 128), 0)
    mine = groups == wanted >> 6
    rows = []
    for c in range(6):
        part = found[N_GROUP * c : N_GROUP * c + N_GROUP]
        rows.append(jnp.sum(jnp.where(mine, part, 0.0), axis=0, keepdims=True))
    return jnp.concatenate(rows + [jnp.zeros((2, 128), jnp.float32)], axis=0)


def far_kernel(last, *refs):
    if last:
        far_ref, mine_ref, self_ref, sum_ref, moment_ref, *outs, mats = refs
    else:
        core_ref, far_ref, mine_ref, self_ref, sum_ref, moment_ref, *outs, early_ref, mats, wide_mats = refs
    rows = far_sources(far_ref, moment_ref)
    blocks = []
    for block in range(2):
        target = self_ref[block, 16:24]
        source = rows[:, 64 * block : 64 * block + 64] - self_ref[block, 24:32][:, 0:64]
        fill_kernels(target, source, mats.at[block], 64)
        sums = sum_ref[block] + weighted_sums(source, mats.at[block], 64)
        new = mine_ref[block, 0:6] + advance_rows(target, sums)
        blocks.append(jnp.concatenate([new, jnp.zeros((2, BS), jnp.float32)], axis=0))
    if last:
        position_ref, strength_ref = outs
        state = jnp.concatenate(blocks, axis=1)
        position_ref[...] = state[0:3]
        strength_ref[...] = state[3:6]
    else:
        publish(blocks, None, *outs)

        @pl.when(core_ref[0] != 0)
        def _():
            own_terms(blocks, early_ref, wide_mats)

        @pl.when(core_ref[0] == 0)
        def _():
            early_ref[...] = jnp.zeros_like(early_ref)


def f32(*shape):
    return jax.ShapeDtypeStruct(shape, jnp.float32)


def kept(*shape):
    return pltpu.VMEM(shape, jnp.float32)


def keep(value):
    return pltpu.with_memory_space_constraint(value, VMEM)


def in_vmem(count):
    return [pl.BlockSpec(memory_space=VMEM)] * count


def in_smem(count):
    return [pl.BlockSpec(memory_space=SMEM)] * count


PUBLISHED = (kept(N_DEV, 1, WIDTH), kept(2, 8, BS))


def pack(pair_list, pair_count, positions, strengths, far_list):
    return pl.pallas_call(
        pack_kernel,
        out_shape=(pltpu.VMEM((1, 128), jnp.int32),) + PUBLISHED,
        in_specs=in_smem(2) + in_vmem(3),
        out_specs=tuple(in_vmem(3)),
        name="pack",
    )(pair_list, pair_count, positions, strengths, far_list.T)


def moments_of(region):
    return pl.pallas_call(
        moment_kernel,
        out_shape=kept(N_GROUP, 1, 6 * REGION_BLOCKS),
        in_specs=in_vmem(1),
        out_specs=in_vmem(1)[0],
        name="moments",
    )(region)


WIDE_MATS = pltpu.VMEM((2, 4, BS, BS), jnp.bfloat16)
SELF_COST = pl.CostEstimate(flops=4000000, bytes_accessed=60000, transcendentals=130000)


def first_self_terms(mine, region):
    return pl.pallas_call(
        first_self_kernel,
        out_shape=(kept(2, 32, BS), pltpu.VMEM((8, 128), jnp.int32)),
        in_specs=in_vmem(2),
        out_specs=tuple(in_vmem(2)),
        scratch_shapes=[WIDE_MATS],
        cost_estimate=SELF_COST,
        name="self_terms",
    )(keep(mine), region)


def later_self_terms(core, mine, early):
    return pl.pallas_call(
        later_self_kernel,
        out_shape=kept(2, 32, BS),
        in_specs=in_smem(1) + in_vmem(2),
        out_specs=in_vmem(1)[0],
        scratch_shapes=[WIDE_MATS],
        cost_estimate=SELF_COST,
        name="self_terms",
    )(core, keep(mine), keep(early))


def near(counts, own, region):
    return pl.pallas_call(
        near_kernel,
        out_shape=kept(2, 16, BS),
        in_specs=in_vmem(3),
        out_specs=in_vmem(1)[0],
        scratch_shapes=[
            pltpu.VMEM((2, 4, BS, BS), jnp.bfloat16),
            pltpu.SMEM((136,), jnp.int32),
            pltpu.SMEM((8, 128), jnp.int32),
            pltpu.SemaphoreType.DMA(()),
        ],
        cost_estimate=pl.CostEstimate(flops=20000000, bytes_accessed=600000, transcendentals=500000),
        name="near",
    )(keep(counts), keep(own), region)


def far(core, far_row, mine, own, sums, moments, last):
    operands = [keep(value) for value in (far_row, mine, own, sums, moments)]
    in_specs = in_vmem(5)
    scratch = [pltpu.VMEM((2, 4, 64, BS), jnp.bfloat16)]
    if last:
        out_shape = (f32(3, 2 * BS), f32(3, 2 * BS))
    else:
        out_shape = PUBLISHED + (kept(2, 32, BS),)
        operands = [core] + operands
        in_specs = in_smem(1) + in_specs
        scratch.append(WIDE_MATS)
    return pl.pallas_call(
        functools.partial(far_kernel, last),
        out_shape=out_shape,
        in_specs=in_specs,
        out_specs=tuple(in_vmem(len(out_shape))),
        scratch_shapes=scratch,
        name="far",
    )(*operands)


def exchange(value, axis):
    return lax.all_to_all(value, axis, 0, 0, tiled=True)


def body(positions, strengths, pair_list, pair_count, far_list):
    core = (lax.axis_index("group").astype(jnp.int32) & (NC - 1)).reshape(1)
    far_row, payload, mine = pack(pair_list, pair_count, positions, strengths, far_list)
    counts, early = None, None
    for step in range(STEPS):
        first, last = step == 0, step == STEPS - 1
        region = keep(exchange(payload, "dev"))
        moments = exchange(moments_of(region), "group")
        if first:
            own, counts = first_self_terms(mine, region)
        else:
            own = later_self_terms(core, mine, early)
        sums = near(counts, own, region)
        result = far(core, far_row, mine, own, sums, moments, last)
        if not last:
            payload, mine, early = result
    return result


def solution(mesh):
    split = P(None, ("group", "dev"))
    return jax.shard_map(
        body,
        mesh=mesh,
        in_specs=(split, split, split, P(("group", "dev")), split),
        out_specs=(split, split),
        check_vma=False,
    )
```

```python
import functools

import jax
import jax.numpy as jnp
from jax import lax
from jax.experimental import pallas as pl
from jax.experimental.pallas import tpu as pltpu
from jax.sharding import PartitionSpec as P

BS = 256
STEPS = 2
NZ, NX, NY, NC = 8, 4, 8, 2
N_DEV = NZ * NX
N_GROUP = NY * NC
REGION_BLOCKS = 2 * N_DEV
CHUNK = 32

INV_FOUR_PI = 0.07957747154594767
CORE_SQUARED = 0.25
TIME_STEP = 0.05

VMEM = pltpu.VMEM
SMEM = pltpu.SMEM


def split_rows(rows):
    high = rows.astype(jnp.bfloat16).astype(jnp.float32)
    rest = rows - high
    middle = rest.astype(jnp.bfloat16).astype(jnp.float32)
    parts = [high, middle, rest - middle, jnp.zeros_like(rows)]
    return jnp.concatenate(parts, axis=0).astype(jnp.bfloat16)


def fill_kernels(target, columns, mats, count):
    tx, ty, tz = target[0:1], target[1:2], target[2:3]
    ax, ay, az = target[3:4], target[4:5], target[5:6]
    for start in range(0, count, CHUNK):
        part = columns[start : start + CHUNK]
        dx = tx - part[:, 0:1]
        dy = ty - part[:, 1:2]
        dz = tz - part[:, 2:3]
        dist_sq = dx * dx + dy * dy + dz * dz + CORE_SQUARED
        inv_root = lax.rsqrt(dist_sq)
        inv_sq = inv_root * inv_root
        first = inv_sq * inv_root
        align = ax * dx + ay * dy + az * dz
        second = first * inv_sq * align
        first_high = first.astype(jnp.bfloat16)
        second_high = second.astype(jnp.bfloat16)
        rows = pl.ds(start, CHUNK)
        mats[0, rows, :] = first_high
        mats[1, rows, :] = (first - first_high.astype(jnp.float32)).astype(jnp.bfloat16)
        mats[2, rows, :] = second_high
        mats[3, rows, :] = (second - second_high.astype(jnp.float32)).astype(jnp.bfloat16)


def weighted_sums(source, mats, count):
    yx, yy, yz = source[0:1], source[1:2], source[2:3]
    bx, by, bz = source[3:4], source[4:5], source[5:6]
    zero = jnp.zeros_like(yx)
    rows = jnp.concatenate(
        [bx, by, bz, yy * bz - yz * by, yz * bx - yx * bz, yx * by - yy * bx, zero, zero], axis=0
    )
    left = split_rows(rows)

    def product(high, low):
        top = jnp.dot(left, mats[high, 0:count, :], preferred_element_type=jnp.float32)
        rest = jnp.dot(left, mats[low, 0:count, :], preferred_element_type=jnp.float32)
        total = top + rest
        return total[0:8] + (total[8:16] + total[16:24])

    return jnp.concatenate([product(0, 1), product(2, 3)], axis=0)


def cross_rows(left, right):
    return jnp.concatenate(
        [
            left[1:2] * right[2:3] - left[2:3] * right[1:2],
            left[2:3] * right[0:1] - left[0:1] * right[2:3],
            left[0:1] * right[1:2] - left[1:2] * right[0:1],
        ],
        axis=0,
    )


def advance_rows(target, sums):
    position, strength = target[0:3], target[3:6]
    velocity = cross_rows(position, sums[0:3]) - sums[3:6]
    twist = cross_rows(strength, sums[0:3])
    spin = cross_rows(position, sums[8:11]) - sums[11:14]
    scale = -INV_FOUR_PI * TIME_STEP
    return scale * jnp.concatenate([velocity, twist - 3.0 * spin], axis=0)


STATE_LANES = 6 * 2 * BS
WIDTH = STATE_LANES + 128


def centre_of(state):
    row = lax.broadcasted_iota(jnp.int32, (8, BS), 0)
    mean = jnp.sum(state, axis=1, keepdims=True) * (1.0 / BS)
    return jnp.where(row < 3, jnp.broadcast_to(mean, (8, BS)), 0.0)


def publish(blocks, info, payload_ref, mine_ref):
    lane = lax.broadcasted_iota(jnp.int32, (8, 128), 1)
    row = lax.broadcasted_iota(jnp.int32, (8, 128), 0)
    table = jnp.zeros((8, 128), jnp.float32)
    for index, block in enumerate(blocks):
        total = jnp.sum(block, axis=1, keepdims=True)
        total = jnp.where(row < 3, total * (1.0 / BS), jnp.broadcast_to(total, (8, 128)))
        table = jnp.where(lane == 8 * index + row, total, table)
        mine_ref[index] = block
    tail = jnp.sum(table, axis=0, keepdims=True)
    if info is not None:
        tail = tail + info
    for device in range(8):
        for c in range(6):
            for index, block in enumerate(blocks):
                payload_ref[device, :, pl.ds(2 * BS * c + BS * index, BS)] = block[c : c + 1]
        payload_ref[device, :, pl.ds(STATE_LANES, 128)] = tail
    for device in range(8, N_DEV, 8):
        payload_ref[device : device + 8] = payload_ref[0:8]
    if info is not None:
        lane = lax.broadcasted_iota(jnp.int32, (1, 128), 1)
        for device in range(N_DEV):
            payload_ref[device, :, pl.ds(STATE_LANES, 128)] = jnp.where(lane == 29, 1.0 * device, tail)


def pack_kernel(pair_ref, count_ref, position_ref, strength_ref, *out_refs):
    zero = jnp.zeros((2, 2 * BS), jnp.float32)
    state = jnp.concatenate([position_ref[...], strength_ref[...], zero], axis=0)
    lane = lax.broadcasted_iota(jnp.int32, (1, 128), 1)
    info = jnp.zeros((1, 128), jnp.int32)
    for side in range(2):
        for slot in range(6):
            info = jnp.where(lane == 16 + 6 * side + slot, pair_ref[side, slot], info)
    info = jnp.where(lane == 28, count_ref[0], info)
    publish([state[:, 0:BS], state[:, BS:]], info.astype(jnp.float32), *out_refs)


def visit_counts(info):
    lane = lax.broadcasted_iota(jnp.int32, (N_DEV, 128), 1)
    first = lane < 22
    partner = jnp.where(first, pltpu.roll(info, 128 - 6, 1), pltpu.roll(info, 6, 1))
    slot = jnp.where(first, lane - 16, lane - 22).astype(jnp.float32)
    own = info - 2.0 * info[:, 29:30]
    live = (slot >= 0.0) & (slot < info[:, 28:29]) & (lane < 28) & (own >= 0.0) & (own < 2.0)
    codes = jnp.where(live, own * 64.0 + partner, -1.0).T
    code = lax.broadcasted_iota(jnp.int32, (128, N_DEV), 0).astype(jnp.float32)
    times = jnp.zeros((128, N_DEV), jnp.float32)
    for row in range(16, 28):
        times = times + jnp.where(code == codes[row : row + 1], 1.0, 0.0)
    counts = lax.dot_general(
        jnp.ones((8, N_DEV), jnp.float32),
        times,
        (((1,), (1,)), ((), ())),
        preferred_element_type=jnp.float32,
    )
    return counts.astype(jnp.int32)


def moment_kernel(region_ref, moment_ref):
    columns = region_ref[:, 0, STATE_LANES:].T
    rows = [columns[8 * t + c : 8 * t + c + 1] for c in range(6) for t in range(2)]
    table = jnp.concatenate(rows, axis=1)
    for group in range(N_GROUP):
        moment_ref[group] = table


def self_kernel(mine_ref, *refs):
    if len(refs) == 2:
        out_ref, mats = refs
    else:
        region_ref, far_ref, out_ref, count_ref, row_ref, mats = refs
        row_ref[...] = jnp.concatenate([far_ref[0:1], far_ref[1:2]], axis=1)
        tails = region_ref[:, 0, STATE_LANES:]
        count_ref[...] = visit_counts(tails)
    for block in range(2):
        state = mine_ref[block]
        centre = centre_of(state)
        target = state - centre
        fill_kernels(target, target.T, mats.at[block], BS)
        out_ref[block, 0:16] = weighted_sums(target, mats.at[block], BS)
        out_ref[block, 16:24] = target
        out_ref[block, 24:32] = centre


def visit_list(count_ref, list_ref):
    def add(code, place):
        times = count_ref[0, code]
        list_ref[place] = times * 128 + code
        return place + jnp.where(times > 0, 1, 0)

    place = lax.fori_loop(0, 128, add, jnp.int32(1), unroll=16)
    list_ref[0] = place - 1


def near_kernel(count_ref, self_ref, region_ref, sum_ref, mats, list_ref, count_smem, sem):
    copy = pltpu.make_async_copy(count_ref, count_smem, sem)
    copy.start()
    copy.wait()
    visit_list(count_smem, list_ref)
    sum_ref[...] = self_ref[:, 0:16]

    def visit(place, slot):
        code = list_ref[place]
        times = (code >> 7).astype(jnp.float32)
        block = (code >> 6) & 1
        source = code & 63
        rows = []
        for c in range(6):
            lanes = pl.ds(pl.multiple_of(2 * BS * c + BS * (source & 1), BS), BS)
            rows.append(region_ref[source >> 1, :, lanes])
        rows.append(jnp.zeros((2, BS), jnp.float32))
        rows = jnp.concatenate(rows, axis=0) - self_ref[block, 24:32]
        fill_kernels(self_ref[block, 16:24], rows.T, mats.at[slot], BS)
        return block, times * weighted_sums(rows, mats.at[slot], BS)

    def visit_two(index, carry):
        block_a, sums_a = visit(2 * index + 1, 0)
        block_b, sums_b = visit(2 * index + 2, 1)
        sum_ref[block_a] += sums_a
        sum_ref[block_b] += sums_b
        return carry

    count = list_ref[0]
    lax.fori_loop(0, count >> 1, visit_two, 0)

    @pl.when(count & 1 == 1)
    def _():
        block, sums = visit(count, 0)
        sum_ref[block] += sums


def far_sources(far_ref, moment_ref):
    table = moment_ref[:, 0, :]
    table = jnp.concatenate(
        [table[:, REGION_BLOCKS * c : REGION_BLOCKS * c + REGION_BLOCKS] for c in range(6)], axis=0
    )
    size = table.shape[0]
    high = table.astype(jnp.bfloat16).astype(jnp.float32)
    middle = (table - high).astype(jnp.bfloat16).astype(jnp.float32)
    parts = jnp.concatenate([high, middle, table - high - middle], axis=0).astype(jnp.bfloat16)
    wanted = far_ref[...]
    place = (wanted & 1) * N_DEV + ((wanted >> 1) & (N_DEV - 1))
    lanes = lax.broadcasted_iota(jnp.int32, (REGION_BLOCKS, 128), 0)
    chosen = jnp.where(lanes == place, 1.0, 0.0).astype(jnp.bfloat16)
    found = jnp.dot(parts, chosen, preferred_element_type=jnp.float32)
    found = found[0:size] + found[size : 2 * size] + found[2 * size :]
    groups = lax.broadcasted_iota(jnp.int32, (N_GROUP, 128), 0)
    mine = groups == wanted >> 6
    rows = []
    for c in range(6):
        part = found[N_GROUP * c : N_GROUP * c + N_GROUP]
        rows.append(jnp.sum(jnp.where(mine, part, 0.0), axis=0, keepdims=True))
    return jnp.concatenate(rows + [jnp.zeros((2, 128), jnp.float32)], axis=0)


def far_kernel(last, far_ref, mine_ref, self_ref, sum_ref, moment_ref, *refs):
    *outs, mats = refs
    centres = [self_ref[block, 24:32][:, 0:64] for block in range(2)]
    rows = far_sources(far_ref, moment_ref) - jnp.concatenate(centres, axis=1)
    columns = rows.T
    blocks = []
    for block in range(2):
        target = self_ref[block, 16:24]
        source = rows[:, 64 * block : 64 * block + 64]
        fill_kernels(target, columns[64 * block : 64 * block + 64], mats.at[block], 64)
        sums = sum_ref[block] + weighted_sums(source, mats.at[block], 64)
        new = mine_ref[block, 0:6] + advance_rows(target, sums)
        blocks.append(jnp.concatenate([new, jnp.zeros((2, BS), jnp.float32)], axis=0))
    if last:
        position_ref, strength_ref = outs
        state = jnp.concatenate(blocks, axis=1)
        position_ref[...] = state[0:3]
        strength_ref[...] = state[3:6]
    else:
        publish(blocks, None, *outs)


def f32(*shape):
    return jax.ShapeDtypeStruct(shape, jnp.float32)


def kept(*shape):
    return pltpu.VMEM(shape, jnp.float32)


def keep(value):
    return pltpu.with_memory_space_constraint(value, VMEM)


def in_vmem(count):
    return [pl.BlockSpec(memory_space=VMEM)] * count


def in_smem(count):
    return [pl.BlockSpec(memory_space=SMEM)] * count


PUBLISHED = (kept(N_DEV, 1, WIDTH), kept(2, 8, BS))


def pack(pair_list, pair_count, positions, strengths):
    return pl.pallas_call(
        pack_kernel,
        out_shape=PUBLISHED,
        in_specs=in_smem(2) + in_vmem(2),
        out_specs=tuple(in_vmem(2)),
        name="pack",
    )(pair_list, pair_count, positions, strengths)


def moments_of(region):
    return pl.pallas_call(
        moment_kernel,
        out_shape=kept(N_GROUP, 1, 6 * REGION_BLOCKS),
        in_specs=in_vmem(1),
        out_specs=in_vmem(1)[0],
        name="moments",
    )(region)


def self_terms(mine, *pair_operands):
    out_shape, out_specs, in_specs = (kept(2, 32, BS),), in_vmem(1), in_vmem(1)
    if pair_operands:
        out_shape += (pltpu.VMEM((8, 128), jnp.int32), pltpu.VMEM((1, 128), jnp.int32))
        out_specs = in_vmem(3)
        in_specs = in_vmem(3)
    return pl.pallas_call(
        self_kernel,
        out_shape=out_shape,
        in_specs=in_specs,
        out_specs=tuple(out_specs),
        scratch_shapes=[pltpu.VMEM((2, 4, BS, BS), jnp.bfloat16)],
        cost_estimate=pl.CostEstimate(flops=4000000, bytes_accessed=60000, transcendentals=130000),
        name="self_terms",
    )(keep(mine), *pair_operands)


def near(counts, own, region):
    return pl.pallas_call(
        near_kernel,
        out_shape=kept(2, 16, BS),
        in_specs=in_vmem(3),
        out_specs=in_vmem(1)[0],
        scratch_shapes=[
            pltpu.VMEM((2, 4, BS, BS), jnp.bfloat16),
            pltpu.SMEM((136,), jnp.int32),
            pltpu.SMEM((8, 128), jnp.int32),
            pltpu.SemaphoreType.DMA(()),
        ],
        cost_estimate=pl.CostEstimate(flops=20000000, bytes_accessed=600000, transcendentals=500000),
        name="near",
    )(keep(counts), keep(own), region)


def far(far_row, mine, own, sums, moments, last):
    out_shape = (f32(3, 2 * BS), f32(3, 2 * BS)) if last else PUBLISHED
    return pl.pallas_call(
        functools.partial(far_kernel, last),
        out_shape=out_shape,
        in_specs=in_vmem(5),
        out_specs=tuple(in_vmem(len(out_shape))),
        scratch_shapes=[pltpu.VMEM((2, 4, 64, BS), jnp.bfloat16)],
        name="far",
    )(keep(far_row), keep(mine), keep(own), keep(sums), keep(moments))


def exchange(value, axis):
    return lax.all_to_all(value, axis, 0, 0, tiled=True)


def body(positions, strengths, pair_list, pair_count, far_list):
    payload, mine = pack(pair_list, pair_count, positions, strengths)
    counts = None
    for step in range(STEPS):
        first, last = step == 0, step == STEPS - 1
        region = keep(exchange(payload, "dev"))
        moments = exchange(moments_of(region), "group")
        if first:
            own, counts, far_row = self_terms(mine, region, far_list.T)
        else:
            (own,) = self_terms(mine)
        sums = near(counts, own, region)
        result = far(far_row, mine, own, sums, moments, last)
        if not last:
            payload, mine = result
    return result


def solution(mesh):
    split = P(None, ("group", "dev"))
    return jax.shard_map(
        body,
        mesh=mesh,
        in_specs=(split, split, split, P(("group", "dev")), split),
        out_specs=(split, split),
        check_vma=False,
    )
```

```python
import functools

import jax
import jax.numpy as jnp
from jax import lax
from jax.experimental import pallas as pl
from jax.experimental.pallas import tpu as pltpu
from jax.sharding import PartitionSpec as P

BS = 256
STEPS = 2
NZ, NX, NY, NC = 8, 4, 8, 2
N_DEV = NZ * NX
N_GROUP = NY * NC
REGION_BLOCKS = 2 * N_DEV
CHUNK = 32

INV_FOUR_PI = 0.07957747154594767
CORE_SQUARED = 0.25
TIME_STEP = 0.05

VMEM = pltpu.VMEM
SMEM = pltpu.SMEM


def split_rows(rows):
    high = rows.astype(jnp.bfloat16).astype(jnp.float32)
    rest = rows - high
    middle = rest.astype(jnp.bfloat16).astype(jnp.float32)
    parts = [high, middle, rest - middle, jnp.zeros_like(rows)]
    return jnp.concatenate(parts, axis=0).astype(jnp.bfloat16)


def fill_kernels(target, columns, mats, count):
    tx, ty, tz = target[0:1], target[1:2], target[2:3]
    ax, ay, az = target[3:4], target[4:5], target[5:6]
    for start in range(0, count, CHUNK):
        part = columns[start : start + CHUNK]
        dx = tx - part[:, 0:1]
        dy = ty - part[:, 1:2]
        dz = tz - part[:, 2:3]
        dist_sq = dx * dx + dy * dy + dz * dz + CORE_SQUARED
        inv_root = lax.rsqrt(dist_sq)
        inv_sq = inv_root * inv_root
        first = inv_sq * inv_root
        align = ax * dx + ay * dy + az * dz
        second = first * inv_sq * align
        first_high = first.astype(jnp.bfloat16)
        second_high = second.astype(jnp.bfloat16)
        rows = pl.ds(start, CHUNK)
        mats[0, rows, :] = first_high
        mats[1, rows, :] = (first - first_high.astype(jnp.float32)).astype(jnp.bfloat16)
        mats[2, rows, :] = second_high
        mats[3, rows, :] = (second - second_high.astype(jnp.float32)).astype(jnp.bfloat16)


def weighted_sums(source, mats, count):
    yx, yy, yz = source[0:1], source[1:2], source[2:3]
    bx, by, bz = source[3:4], source[4:5], source[5:6]
    zero = jnp.zeros_like(yx)
    rows = jnp.concatenate(
        [bx, by, bz, yy * bz - yz * by, yz * bx - yx * bz, yx * by - yy * bx, zero, zero], axis=0
    )
    left = split_rows(rows)

    def product(high, low):
        top = jnp.dot(left, mats[high, 0:count, :], preferred_element_type=jnp.float32)
        rest = jnp.dot(left, mats[low, 0:count, :], preferred_element_type=jnp.float32)
        total = top + rest
        return total[0:8] + (total[8:16] + total[16:24])

    return jnp.concatenate([product(0, 1), product(2, 3)], axis=0)


def cross_rows(left, right):
    return jnp.concatenate(
        [
            left[1:2] * right[2:3] - left[2:3] * right[1:2],
            left[2:3] * right[0:1] - left[0:1] * right[2:3],
            left[0:1] * right[1:2] - left[1:2] * right[0:1],
        ],
        axis=0,
    )


def advance_rows(target, sums):
    position, strength = target[0:3], target[3:6]
    velocity = cross_rows(position, sums[0:3]) - sums[3:6]
    twist = cross_rows(strength, sums[0:3])
    spin = cross_rows(position, sums[8:11]) - sums[11:14]
    scale = -INV_FOUR_PI * TIME_STEP
    return scale * jnp.concatenate([velocity, twist - 3.0 * spin], axis=0)


STATE_LANES = 6 * 2 * BS
WIDTH = STATE_LANES + 128


def centre_of(state):
    row = lax.broadcasted_iota(jnp.int32, (8, BS), 0)
    mean = jnp.sum(state, axis=1, keepdims=True) * (1.0 / BS)
    return jnp.where(row < 3, jnp.broadcast_to(mean, (8, BS)), 0.0)


def publish(blocks, info, payload_ref, mine_ref):
    lane = lax.broadcasted_iota(jnp.int32, (8, 128), 1)
    row = lax.broadcasted_iota(jnp.int32, (8, 128), 0)
    table = jnp.zeros((8, 128), jnp.float32)
    for index, block in enumerate(blocks):
        total = jnp.sum(block, axis=1, keepdims=True)
        total = jnp.where(row < 3, total * (1.0 / BS), jnp.broadcast_to(total, (8, 128)))
        table = jnp.where(lane == 8 * index + row, total, table)
        mine_ref[index] = block
    tail = jnp.sum(table, axis=0, keepdims=True)
    if info is not None:
        tail = tail + info
    for device in range(8):
        for c in range(6):
            for index, block in enumerate(blocks):
                payload_ref[device, :, pl.ds(2 * BS * c + BS * index, BS)] = block[c : c + 1]
        payload_ref[device, :, pl.ds(STATE_LANES, 128)] = tail
    for device in range(8, N_DEV, 8):
        payload_ref[device : device + 8] = payload_ref[0:8]
    if info is not None:
        lane = lax.broadcasted_iota(jnp.int32, (1, 128), 1)
        for device in range(N_DEV):
            payload_ref[device, :, pl.ds(STATE_LANES, 128)] = jnp.where(lane == 29, 1.0 * device, tail)


def pack_kernel(pair_ref, count_ref, position_ref, strength_ref, *out_refs):
    zero = jnp.zeros((2, 2 * BS), jnp.float32)
    state = jnp.concatenate([position_ref[...], strength_ref[...], zero], axis=0)
    info = jnp.concatenate(
        [
            jnp.zeros((1, 16), jnp.int32),
            pair_ref[0:1],
            pair_ref[1:2],
            count_ref[...],
            jnp.zeros((1, 99), jnp.int32),
        ],
        axis=1,
    )
    publish([state[:, 0:BS], state[:, BS:]], info.astype(jnp.float32), *out_refs)


def visit_counts(info):
    lane = lax.broadcasted_iota(jnp.int32, (N_DEV, 128), 1)
    first = lane < 22
    partner = jnp.where(first, pltpu.roll(info, 128 - 6, 1), pltpu.roll(info, 6, 1))
    slot = jnp.where(first, lane - 16, lane - 22).astype(jnp.float32)
    own = info - 2.0 * info[:, 29:30]
    live = (slot >= 0.0) & (slot < info[:, 28:29]) & (lane < 28) & (own >= 0.0) & (own < 2.0)
    codes = jnp.where(live, own * 64.0 + partner, -1.0).T
    code = lax.broadcasted_iota(jnp.int32, (128, N_DEV), 0).astype(jnp.float32)
    times = jnp.zeros((128, N_DEV), jnp.float32)
    for row in range(16, 28):
        times = times + jnp.where(code == codes[row : row + 1], 1.0, 0.0)
    counts = lax.dot_general(
        jnp.ones((8, N_DEV), jnp.float32),
        times,
        (((1,), (1,)), ((), ())),
        preferred_element_type=jnp.float32,
    )
    return counts.astype(jnp.int32)


def moment_kernel(region_ref, moment_ref):
    columns = region_ref[:, 0, STATE_LANES:].T
    rows = [columns[8 * t + c : 8 * t + c + 1] for c in range(6) for t in range(2)]
    table = jnp.concatenate(rows, axis=1)
    for group in range(N_GROUP):
        moment_ref[group] = table


def self_kernel(mine_ref, *refs):
    if len(refs) == 2:
        out_ref, mats = refs
    else:
        region_ref, far_ref, out_ref, count_ref, row_ref, mats = refs
        row_ref[...] = jnp.concatenate([far_ref[0:1], far_ref[1:2]], axis=1)
        tails = region_ref[:, 0, STATE_LANES:]
        count_ref[...] = visit_counts(tails)
    for block in range(2):
        state = mine_ref[block]
        centre = centre_of(state)
        target = state - centre
        fill_kernels(target, target.T, mats.at[block], BS)
        out_ref[block, 0:16] = weighted_sums(target, mats.at[block], BS)
        out_ref[block, 16:24] = target
        out_ref[block, 24:32] = centre


def visit_list(count_ref, list_ref):
    def add(code, place):
        times = count_ref[0, code]
        list_ref[place] = times * 128 + code
        return place + jnp.where(times > 0, 1, 0)

    place = lax.fori_loop(0, 128, add, jnp.int32(1), unroll=16)
    list_ref[0] = place - 1


def near_kernel(count_ref, self_ref, region_ref, sum_ref, mats, list_ref, count_smem, sem):
    copy = pltpu.make_async_copy(count_ref, count_smem, sem)
    copy.start()
    copy.wait()
    visit_list(count_smem, list_ref)
    sum_ref[...] = self_ref[:, 0:16]

    def visit(place, slot):
        code = list_ref[place]
        times = (code >> 7).astype(jnp.float32)
        block = (code >> 6) & 1
        source = code & 63
        rows = []
        for c in range(6):
            lanes = pl.ds(pl.multiple_of(2 * BS * c + BS * (source & 1), BS), BS)
            rows.append(region_ref[source >> 1, :, lanes])
        rows.append(jnp.zeros((2, BS), jnp.float32))
        rows = jnp.concatenate(rows, axis=0) - self_ref[block, 24:32]
        fill_kernels(self_ref[block, 16:24], rows.T, mats.at[slot], BS)
        return block, times * weighted_sums(rows, mats.at[slot], BS)

    def visit_two(index, carry):
        block_a, sums_a = visit(2 * index + 1, 0)
        block_b, sums_b = visit(2 * index + 2, 1)
        sum_ref[block_a] += sums_a
        sum_ref[block_b] += sums_b
        return carry

    count = list_ref[0]
    lax.fori_loop(0, count >> 1, visit_two, 0)

    @pl.when(count & 1 == 1)
    def _():
        block, sums = visit(count, 0)
        sum_ref[block] += sums


def far_sources(far_ref, moment_ref):
    table = moment_ref[:, 0, :]
    table = jnp.concatenate(
        [table[:, REGION_BLOCKS * c : REGION_BLOCKS * c + REGION_BLOCKS] for c in range(6)], axis=0
    )
    size = table.shape[0]
    high = table.astype(jnp.bfloat16).astype(jnp.float32)
    middle = (table - high).astype(jnp.bfloat16).astype(jnp.float32)
    parts = jnp.concatenate([high, middle, table - high - middle], axis=0).astype(jnp.bfloat16)
    wanted = far_ref[...]
    place = (wanted & 1) * N_DEV + ((wanted >> 1) & (N_DEV - 1))
    lanes = lax.broadcasted_iota(jnp.int32, (REGION_BLOCKS, 128), 0)
    chosen = jnp.where(lanes == place, 1.0, 0.0).astype(jnp.bfloat16)
    found = jnp.dot(parts, chosen, preferred_element_type=jnp.float32)
    found = found[0:size] + found[size : 2 * size] + found[2 * size :]
    groups = lax.broadcasted_iota(jnp.int32, (N_GROUP, 128), 0)
    mine = groups == wanted >> 6
    rows = []
    for c in range(6):
        part = found[N_GROUP * c : N_GROUP * c + N_GROUP]
        rows.append(jnp.sum(jnp.where(mine, part, 0.0), axis=0, keepdims=True))
    return jnp.concatenate(rows + [jnp.zeros((2, 128), jnp.float32)], axis=0)


def far_kernel(last, far_ref, mine_ref, self_ref, sum_ref, moment_ref, *refs):
    *outs, mats = refs
    centres = [self_ref[block, 24:32][:, 0:64] for block in range(2)]
    rows = far_sources(far_ref, moment_ref) - jnp.concatenate(centres, axis=1)
    columns = rows.T
    blocks = []
    for block in range(2):
        target = self_ref[block, 16:24]
        source = rows[:, 64 * block : 64 * block + 64]
        fill_kernels(target, columns[64 * block : 64 * block + 64], mats.at[block], 64)
        sums = sum_ref[block] + weighted_sums(source, mats.at[block], 64)
        new = mine_ref[block, 0:6] + advance_rows(target, sums)
        blocks.append(jnp.concatenate([new, jnp.zeros((2, BS), jnp.float32)], axis=0))
    if last:
        position_ref, strength_ref = outs
        state = jnp.concatenate(blocks, axis=1)
        position_ref[...] = state[0:3]
        strength_ref[...] = state[3:6]
    else:
        publish(blocks, None, *outs)


def f32(*shape):
    return jax.ShapeDtypeStruct(shape, jnp.float32)


def kept(*shape):
    return pltpu.VMEM(shape, jnp.float32)


def keep(value):
    return pltpu.with_memory_space_constraint(value, VMEM)


def in_vmem(count):
    return [pl.BlockSpec(memory_space=VMEM)] * count


def in_smem(count):
    return [pl.BlockSpec(memory_space=SMEM)] * count


PUBLISHED = (kept(N_DEV, 1, WIDTH), kept(2, 8, BS))


def pack(pair_list, pair_count, positions, strengths):
    return pl.pallas_call(
        pack_kernel,
        out_shape=PUBLISHED,
        in_specs=in_vmem(4),
        out_specs=tuple(in_vmem(2)),
        name="pack",
    )(pair_list, pair_count.reshape(1, 1), positions, strengths)


def moments_of(region):
    return pl.pallas_call(
        moment_kernel,
        out_shape=kept(N_GROUP, 1, 6 * REGION_BLOCKS),
        in_specs=in_vmem(1),
        out_specs=in_vmem(1)[0],
        name="moments",
    )(region)


def self_terms(mine, *pair_operands):
    out_shape, out_specs, in_specs = (kept(2, 32, BS),), in_vmem(1), in_vmem(1)
    if pair_operands:
        out_shape += (pltpu.VMEM((8, 128), jnp.int32), pltpu.VMEM((1, 128), jnp.int32))
        out_specs = in_vmem(3)
        in_specs = in_vmem(3)
    return pl.pallas_call(
        self_kernel,
        out_shape=out_shape,
        in_specs=in_specs,
        out_specs=tuple(out_specs),
        scratch_shapes=[pltpu.VMEM((2, 4, BS, BS), jnp.bfloat16)],
        cost_estimate=pl.CostEstimate(flops=4000000, bytes_accessed=60000, transcendentals=130000),
        name="self_terms",
    )(keep(mine), *pair_operands)


def near(counts, own, region):
    return pl.pallas_call(
        near_kernel,
        out_shape=kept(2, 16, BS),
        in_specs=in_vmem(3),
        out_specs=in_vmem(1)[0],
        scratch_shapes=[
            pltpu.VMEM((2, 4, BS, BS), jnp.bfloat16),
            pltpu.SMEM((136,), jnp.int32),
            pltpu.SMEM((8, 128), jnp.int32),
            pltpu.SemaphoreType.DMA(()),
        ],
        cost_estimate=pl.CostEstimate(flops=20000000, bytes_accessed=600000, transcendentals=500000),
        name="near",
    )(keep(counts), keep(own), region)


def far(far_row, mine, own, sums, moments, last):
    out_shape = (f32(3, 2 * BS), f32(3, 2 * BS)) if last else PUBLISHED
    return pl.pallas_call(
        functools.partial(far_kernel, last),
        out_shape=out_shape,
        in_specs=in_vmem(5),
        out_specs=tuple(in_vmem(len(out_shape))),
        scratch_shapes=[pltpu.VMEM((2, 4, 64, BS), jnp.bfloat16)],
        name="far",
    )(keep(far_row), keep(mine), keep(own), keep(sums), keep(moments))


def exchange(value, axis):
    return lax.all_to_all(value, axis, 0, 0, tiled=True)


def body(positions, strengths, pair_list, pair_count, far_list):
    payload, mine = pack(pair_list, pair_count, positions, strengths)
    counts = None
    for step in range(STEPS):
        first, last = step == 0, step == STEPS - 1
        region = keep(exchange(payload, "dev"))
        moments = exchange(moments_of(region), "group")
        if first:
            own, counts, far_row = self_terms(mine, region, far_list.T)
        else:
            (own,) = self_terms(mine)
        sums = near(counts, own, region)
        result = far(far_row, mine, own, sums, moments, last)
        if not last:
            payload, mine = result
    return result


def solution(mesh):
    split = P(None, ("group", "dev"))
    return jax.shard_map(
        body,
        mesh=mesh,
        in_specs=(split, split, split, P(("group", "dev")), split),
        out_specs=(split, split),
        check_vma=False,
    )
```

```python
import functools

import jax
import jax.numpy as jnp
from jax import lax
from jax.experimental import pallas as pl
from jax.experimental.pallas import tpu as pltpu
from jax.sharding import PartitionSpec as P

BS = 256
STEPS = 2
NZ, NX, NY, NC = 8, 4, 8, 2
N_DEV = NZ * NX
N_GROUP = NY * NC
REGION_BLOCKS = 2 * N_DEV
CHUNK = 32

INV_FOUR_PI = 0.07957747154594767
CORE_SQUARED = 0.25
TIME_STEP = 0.05

VMEM = pltpu.VMEM
SMEM = pltpu.SMEM


def split_rows(rows):
    high = rows.astype(jnp.bfloat16).astype(jnp.float32)
    rest = rows - high
    middle = rest.astype(jnp.bfloat16).astype(jnp.float32)
    parts = [high, middle, rest - middle, jnp.zeros_like(rows)]
    return jnp.concatenate(parts, axis=0).astype(jnp.bfloat16)


def fill_kernels(target, columns, mats, count):
    tx, ty, tz = target[0:1], target[1:2], target[2:3]
    ax, ay, az = target[3:4], target[4:5], target[5:6]
    for start in range(0, count, CHUNK):
        part = columns[start : start + CHUNK]
        dx = tx - part[:, 0:1]
        dy = ty - part[:, 1:2]
        dz = tz - part[:, 2:3]
        dist_sq = dx * dx + dy * dy + dz * dz + CORE_SQUARED
        inv_root = lax.rsqrt(dist_sq)
        inv_sq = inv_root * inv_root
        first = inv_sq * inv_root
        align = ax * dx + ay * dy + az * dz
        second = first * inv_sq * align
        first_high = first.astype(jnp.bfloat16)
        second_high = second.astype(jnp.bfloat16)
        rows = pl.ds(start, CHUNK)
        mats[0, rows, :] = first_high
        mats[1, rows, :] = (first - first_high.astype(jnp.float32)).astype(jnp.bfloat16)
        mats[2, rows, :] = second_high
        mats[3, rows, :] = (second - second_high.astype(jnp.float32)).astype(jnp.bfloat16)


def weighted_sums(source, mats, count):
    yx, yy, yz = source[0:1], source[1:2], source[2:3]
    bx, by, bz = source[3:4], source[4:5], source[5:6]
    zero = jnp.zeros_like(yx)
    rows = jnp.concatenate(
        [bx, by, bz, yy * bz - yz * by, yz * bx - yx * bz, yx * by - yy * bx, zero, zero], axis=0
    )
    left = split_rows(rows)

    def product(high, low):
        top = jnp.dot(left, mats[high, 0:count, :], preferred_element_type=jnp.float32)
        rest = jnp.dot(left, mats[low, 0:count, :], preferred_element_type=jnp.float32)
        total = top + rest
        return total[0:8] + (total[8:16] + total[16:24])

    return jnp.concatenate([product(0, 1), product(2, 3)], axis=0)


def cross_rows(left, right):
    return jnp.concatenate(
        [
            left[1:2] * right[2:3] - left[2:3] * right[1:2],
            left[2:3] * right[0:1] - left[0:1] * right[2:3],
            left[0:1] * right[1:2] - left[1:2] * right[0:1],
        ],
        axis=0,
    )


def advance_rows(target, sums):
    position, strength = target[0:3], target[3:6]
    velocity = cross_rows(position, sums[0:3]) - sums[3:6]
    twist = cross_rows(strength, sums[0:3])
    spin = cross_rows(position, sums[8:11]) - sums[11:14]
    scale = -INV_FOUR_PI * TIME_STEP
    return scale * jnp.concatenate([velocity, twist - 3.0 * spin], axis=0)


STATE_LANES = 6 * 2 * BS
WIDTH = STATE_LANES + 128


def centre_of(state):
    row = lax.broadcasted_iota(jnp.int32, (8, BS), 0)
    mean = jnp.sum(state, axis=1, keepdims=True) * (1.0 / BS)
    return jnp.where(row < 3, jnp.broadcast_to(mean, (8, BS)), 0.0)


def publish(blocks, info, payload_ref, mine_ref):
    lane = lax.broadcasted_iota(jnp.int32, (8, 128), 1)
    row = lax.broadcasted_iota(jnp.int32, (8, 128), 0)
    table = jnp.zeros((8, 128), jnp.float32)
    for index, block in enumerate(blocks):
        total = jnp.sum(block, axis=1, keepdims=True)
        total = jnp.where(row < 3, total * (1.0 / BS), jnp.broadcast_to(total, (8, 128)))
        table = jnp.where(lane == 8 * index + row, total, table)
        mine_ref[index] = block
    tail = jnp.sum(table, axis=0, keepdims=True)
    if info is not None:
        tail = tail + info
    for device in range(8):
        for c in range(6):
            for index, block in enumerate(blocks):
                payload_ref[device, :, pl.ds(2 * BS * c + BS * index, BS)] = block[c : c + 1]
        payload_ref[device, :, pl.ds(STATE_LANES, 128)] = tail
    for device in range(8, N_DEV, 8):
        payload_ref[device : device + 8] = payload_ref[0:8]
    if info is not None:
        lane = lax.broadcasted_iota(jnp.int32, (1, 128), 1)
        for device in range(N_DEV):
            payload_ref[device, :, pl.ds(STATE_LANES, 128)] = jnp.where(lane == 29, 1.0 * device, tail)


def pack_kernel(pair_ref, count_ref, position_ref, strength_ref, far_ref, row_ref, *out_refs):
    row_ref[...] = jnp.concatenate([far_ref[0:1], far_ref[1:2]], axis=1)
    zero = jnp.zeros((2, 2 * BS), jnp.float32)
    state = jnp.concatenate([position_ref[...], strength_ref[...], zero], axis=0)
    lane = lax.broadcasted_iota(jnp.int32, (1, 128), 1)
    info = jnp.zeros((1, 128), jnp.int32)
    for side in range(2):
        for slot in range(6):
            info = jnp.where(lane == 16 + 6 * side + slot, pair_ref[side, slot], info)
    info = jnp.where(lane == 28, count_ref[0], info)
    publish([state[:, 0:BS], state[:, BS:]], info.astype(jnp.float32), *out_refs)


def visit_counts(info):
    lane = lax.broadcasted_iota(jnp.int32, (N_DEV, 128), 1)
    first = lane < 22
    partner = jnp.where(first, pltpu.roll(info, 128 - 6, 1), pltpu.roll(info, 6, 1))
    slot = jnp.where(first, lane - 16, lane - 22).astype(jnp.float32)
    own = info - 2.0 * info[:, 29:30]
    live = (slot >= 0.0) & (slot < info[:, 28:29]) & (lane < 28) & (own >= 0.0) & (own < 2.0)
    codes = jnp.where(live, own * 64.0 + partner, -1.0).T
    code = lax.broadcasted_iota(jnp.int32, (128, N_DEV), 0).astype(jnp.float32)
    times = jnp.zeros((128, N_DEV), jnp.float32)
    for row in range(16, 28):
        times = times + jnp.where(code == codes[row : row + 1], 1.0, 0.0)
    counts = lax.dot_general(
        jnp.ones((8, N_DEV), jnp.float32),
        times,
        (((1,), (1,)), ((), ())),
        preferred_element_type=jnp.float32,
    )
    return counts.astype(jnp.int32)


def moment_kernel(region_ref, moment_ref):
    columns = region_ref[:, 0, STATE_LANES:].T
    rows = [columns[8 * t + c : 8 * t + c + 1] for c in range(6) for t in range(2)]
    table = jnp.concatenate(rows, axis=1)
    for group in range(N_GROUP):
        moment_ref[group] = table


def self_kernel(mine_ref, *refs):
    if len(refs) == 2:
        out_ref, mats = refs
    else:
        region_ref, out_ref, count_ref, mats = refs
        tails = region_ref[:, 0, STATE_LANES:]
        count_ref[...] = visit_counts(tails)
    for block in range(2):
        state = mine_ref[block]
        centre = centre_of(state)
        target = state - centre
        fill_kernels(target, target.T, mats.at[block], BS)
        out_ref[block, 0:16] = weighted_sums(target, mats.at[block], BS)
        out_ref[block, 16:24] = target
        out_ref[block, 24:32] = centre


def visit_list(count_ref, list_ref):
    def add(code, place):
        times = count_ref[0, code]
        list_ref[place] = times * 128 + code
        return place + jnp.where(times > 0, 1, 0)

    place = lax.fori_loop(0, 128, add, jnp.int32(1), unroll=16)
    list_ref[0] = place - 1


def near_kernel(count_ref, self_ref, region_ref, sum_ref, mats, list_ref, count_smem, sem):
    copy = pltpu.make_async_copy(count_ref, count_smem, sem)
    copy.start()
    copy.wait()
    visit_list(count_smem, list_ref)
    sum_ref[...] = self_ref[:, 0:16]

    def visit(place, slot):
        code = list_ref[place]
        times = (code >> 7).astype(jnp.float32)
        block = (code >> 6) & 1
        source = code & 63
        rows = []
        for c in range(6):
            lanes = pl.ds(pl.multiple_of(2 * BS * c + BS * (source & 1), BS), BS)
            rows.append(region_ref[source >> 1, :, lanes])
        rows.append(jnp.zeros((2, BS), jnp.float32))
        rows = jnp.concatenate(rows, axis=0) - self_ref[block, 24:32]
        fill_kernels(self_ref[block, 16:24], rows.T, mats.at[slot], BS)
        return block, times * weighted_sums(rows, mats.at[slot], BS)

    def visit_two(index, carry):
        block_a, sums_a = visit(2 * index + 1, 0)
        block_b, sums_b = visit(2 * index + 2, 1)
        sum_ref[block_a] += sums_a
        sum_ref[block_b] += sums_b
        return carry

    count = list_ref[0]
    lax.fori_loop(0, count >> 1, visit_two, 0)

    @pl.when(count & 1 == 1)
    def _():
        block, sums = visit(count, 0)
        sum_ref[block] += sums


def far_sources(far_ref, moment_ref):
    table = moment_ref[:, 0, :]
    table = jnp.concatenate(
        [table[:, REGION_BLOCKS * c : REGION_BLOCKS * c + REGION_BLOCKS] for c in range(6)], axis=0
    )
    size = table.shape[0]
    high = table.astype(jnp.bfloat16).astype(jnp.float32)
    middle = (table - high).astype(jnp.bfloat16).astype(jnp.float32)
    parts = jnp.concatenate([high, middle, table - high - middle], axis=0).astype(jnp.bfloat16)
    wanted = far_ref[...]
    place = (wanted & 1) * N_DEV + ((wanted >> 1) & (N_DEV - 1))
    lanes = lax.broadcasted_iota(jnp.int32, (REGION_BLOCKS, 128), 0)
    chosen = jnp.where(lanes == place, 1.0, 0.0).astype(jnp.bfloat16)
    found = jnp.dot(parts, chosen, preferred_element_type=jnp.float32)
    found = found[0:size] + found[size : 2 * size] + found[2 * size :]
    groups = lax.broadcasted_iota(jnp.int32, (N_GROUP, 128), 0)
    mine = groups == wanted >> 6
    rows = []
    for c in range(6):
        part = found[N_GROUP * c : N_GROUP * c + N_GROUP]
        rows.append(jnp.sum(jnp.where(mine, part, 0.0), axis=0, keepdims=True))
    return jnp.concatenate(rows + [jnp.zeros((2, 128), jnp.float32)], axis=0)


def far_kernel(last, far_ref, mine_ref, self_ref, sum_ref, moment_ref, *refs):
    *outs, mats = refs
    centres = [self_ref[block, 24:32][:, 0:64] for block in range(2)]
    rows = far_sources(far_ref, moment_ref) - jnp.concatenate(centres, axis=1)
    columns = rows.T
    blocks = []
    for block in range(2):
        target = self_ref[block, 16:24]
        source = rows[:, 64 * block : 64 * block + 64]
        fill_kernels(target, columns[64 * block : 64 * block + 64], mats.at[block], 64)
        sums = sum_ref[block] + weighted_sums(source, mats.at[block], 64)
        new = mine_ref[block, 0:6] + advance_rows(target, sums)
        blocks.append(jnp.concatenate([new, jnp.zeros((2, BS), jnp.float32)], axis=0))
    if last:
        position_ref, strength_ref = outs
        state = jnp.concatenate(blocks, axis=1)
        position_ref[...] = state[0:3]
        strength_ref[...] = state[3:6]
    else:
        publish(blocks, None, *outs)


def f32(*shape):
    return jax.ShapeDtypeStruct(shape, jnp.float32)


def kept(*shape):
    return pltpu.VMEM(shape, jnp.float32)


def keep(value):
    return pltpu.with_memory_space_constraint(value, VMEM)


def in_vmem(count):
    return [pl.BlockSpec(memory_space=VMEM)] * count


def in_smem(count):
    return [pl.BlockSpec(memory_space=SMEM)] * count


PUBLISHED = (kept(N_DEV, 1, WIDTH), kept(2, 8, BS))


def pack(pair_list, pair_count, positions, strengths, far_list):
    return pl.pallas_call(
        pack_kernel,
        out_shape=(pltpu.VMEM((1, 128), jnp.int32),) + PUBLISHED,
        in_specs=in_smem(2) + in_vmem(3),
        out_specs=tuple(in_vmem(3)),
        name="pack",
    )(pair_list, pair_count, positions, strengths, far_list.T)


def moments_of(region):
    return pl.pallas_call(
        moment_kernel,
        out_shape=kept(N_GROUP, 1, 6 * REGION_BLOCKS),
        in_specs=in_vmem(1),
        out_specs=in_vmem(1)[0],
        name="moments",
    )(region)


def self_terms(mine, *pair_operands):
    out_shape, out_specs, in_specs = (kept(2, 32, BS),), in_vmem(1), in_vmem(1)
    if pair_operands:
        out_shape += (pltpu.VMEM((8, 128), jnp.int32),)
        out_specs = in_vmem(2)
        in_specs = in_vmem(2)
    return pl.pallas_call(
        self_kernel,
        out_shape=out_shape,
        in_specs=in_specs,
        out_specs=tuple(out_specs),
        scratch_shapes=[pltpu.VMEM((2, 4, BS, BS), jnp.bfloat16)],
        cost_estimate=pl.CostEstimate(flops=4000000, bytes_accessed=60000, transcendentals=130000),
        name="self_terms",
    )(keep(mine), *pair_operands)


def near(counts, own, region):
    return pl.pallas_call(
        near_kernel,
        out_shape=kept(2, 16, BS),
        in_specs=in_vmem(3),
        out_specs=in_vmem(1)[0],
        scratch_shapes=[
            pltpu.VMEM((2, 4, BS, BS), jnp.bfloat16),
            pltpu.SMEM((136,), jnp.int32),
            pltpu.SMEM((8, 128), jnp.int32),
            pltpu.SemaphoreType.DMA(()),
        ],
        cost_estimate=pl.CostEstimate(flops=20000000, bytes_accessed=600000, transcendentals=500000),
        name="near",
    )(keep(counts), keep(own), region)


def far(far_row, mine, own, sums, moments, last):
    out_shape = (f32(3, 2 * BS), f32(3, 2 * BS)) if last else PUBLISHED
    return pl.pallas_call(
        functools.partial(far_kernel, last),
        out_shape=out_shape,
        in_specs=in_vmem(5),
        out_specs=tuple(in_vmem(len(out_shape))),
        scratch_shapes=[pltpu.VMEM((2, 4, 64, BS), jnp.bfloat16)],
        name="far",
    )(keep(far_row), keep(mine), keep(own), keep(sums), keep(moments))


def exchange(value, axis):
    return lax.all_to_all(value, axis, 0, 0, tiled=True)


def body(positions, strengths, pair_list, pair_count, far_list):
    far_row, payload, mine = pack(pair_list, pair_count, positions, strengths, far_list)
    counts = None
    for step in range(STEPS):
        first, last = step == 0, step == STEPS - 1
        region = keep(exchange(payload, "dev"))
        moments = exchange(moments_of(region), "group")
        if first:
            own, counts = self_terms(mine, region)
        else:
            (own,) = self_terms(mine)
        sums = near(counts, own, region)
        result = far(far_row, mine, own, sums, moments, last)
        if not last:
            payload, mine = result
    return result


def solution(mesh):
    split = P(None, ("group", "dev"))
    return jax.shard_map(
        body,
        mesh=mesh,
        in_specs=(split, split, split, P(("group", "dev")), split),
        out_specs=(split, split),
        check_vma=False,
    )
```

```python
import functools

import jax
import jax.numpy as jnp
from jax import lax
from jax.experimental import pallas as pl
from jax.experimental.pallas import tpu as pltpu
from jax.sharding import PartitionSpec as P

BS = 256
STEPS = 2
NZ, NX, NY, NC = 8, 4, 8, 2
N_DEV = NZ * NX
N_GROUP = NY * NC
REGION_BLOCKS = 2 * N_DEV
CHUNK = 64

INV_FOUR_PI = 0.07957747154594767
CORE_SQUARED = 0.25
TIME_STEP = 0.05

VMEM = pltpu.VMEM
SMEM = pltpu.SMEM


def split_rows(rows):
    high = rows.astype(jnp.bfloat16).astype(jnp.float32)
    rest = rows - high
    middle = rest.astype(jnp.bfloat16).astype(jnp.float32)
    parts = [high, middle, rest - middle, jnp.zeros_like(rows)]
    return jnp.concatenate(parts, axis=0).astype(jnp.bfloat16)


def fill_kernels(target, columns, mats, count):
    tx, ty, tz = target[0:1], target[1:2], target[2:3]
    ax, ay, az = target[3:4], target[4:5], target[5:6]
    for start in range(0, count, CHUNK):
        part = columns[start : start + CHUNK]
        dx = tx - part[:, 0:1]
        dy = ty - part[:, 1:2]
        dz = tz - part[:, 2:3]
        dist_sq = dx * dx + dy * dy + dz * dz + CORE_SQUARED
        inv_root = lax.rsqrt(dist_sq)
        inv_sq = inv_root * inv_root
        first = inv_sq * inv_root
        align = ax * dx + ay * dy + az * dz
        second = first * inv_sq * align
        first_high = first.astype(jnp.bfloat16)
        second_high = second.astype(jnp.bfloat16)
        rows = pl.ds(start, CHUNK)
        mats[0, rows, :] = first_high
        mats[1, rows, :] = (first - first_high.astype(jnp.float32)).astype(jnp.bfloat16)
        mats[2, rows, :] = second_high
        mats[3, rows, :] = (second - second_high.astype(jnp.float32)).astype(jnp.bfloat16)


def weighted_sums(source, mats, count):
    yx, yy, yz = source[0:1], source[1:2], source[2:3]
    bx, by, bz = source[3:4], source[4:5], source[5:6]
    zero = jnp.zeros_like(yx)
    rows = jnp.concatenate(
        [bx, by, bz, yy * bz - yz * by, yz * bx - yx * bz, yx * by - yy * bx, zero, zero], axis=0
    )
    left = split_rows(rows)

    def product(high, low):
        top = jnp.dot(left, mats[high, 0:count, :], preferred_element_type=jnp.float32)
        rest = jnp.dot(left, mats[low, 0:count, :], preferred_element_type=jnp.float32)
        total = top + rest
        return total[0:8] + (total[8:16] + total[16:24])

    return jnp.concatenate([product(0, 1), product(2, 3)], axis=0)


def cross_rows(left, right):
    return jnp.concatenate(
        [
            left[1:2] * right[2:3] - left[2:3] * right[1:2],
            left[2:3] * right[0:1] - left[0:1] * right[2:3],
            left[0:1] * right[1:2] - left[1:2] * right[0:1],
        ],
        axis=0,
    )


def advance_rows(target, sums):
    position, strength = target[0:3], target[3:6]
    velocity = cross_rows(position, sums[0:3]) - sums[3:6]
    twist = cross_rows(strength, sums[0:3])
    spin = cross_rows(position, sums[8:11]) - sums[11:14]
    scale = -INV_FOUR_PI * TIME_STEP
    return scale * jnp.concatenate([velocity, twist - 3.0 * spin], axis=0)


STATE_LANES = 6 * 2 * BS
WIDTH = STATE_LANES + 128


def centre_of(state):
    row = lax.broadcasted_iota(jnp.int32, (8, BS), 0)
    mean = jnp.sum(state, axis=1, keepdims=True) * (1.0 / BS)
    return jnp.where(row < 3, jnp.broadcast_to(mean, (8, BS)), 0.0)


def publish(blocks, info, payload_ref, mine_ref):
    lane = lax.broadcasted_iota(jnp.int32, (8, 128), 1)
    row = lax.broadcasted_iota(jnp.int32, (8, 128), 0)
    table = jnp.zeros((8, 128), jnp.float32)
    for index, block in enumerate(blocks):
        total = jnp.sum(block, axis=1, keepdims=True)
        total = jnp.where(row < 3, total * (1.0 / BS), jnp.broadcast_to(total, (8, 128)))
        table = jnp.where(lane == 8 * index + row, total, table)
        mine_ref[index] = block
    tail = jnp.sum(table, axis=0, keepdims=True)
    if info is not None:
        tail = tail + info
    for device in range(8):
        for c in range(6):
            for index, block in enumerate(blocks):
                payload_ref[device, :, pl.ds(2 * BS * c + BS * index, BS)] = block[c : c + 1]
        payload_ref[device, :, pl.ds(STATE_LANES, 128)] = tail
    for device in range(8, N_DEV, 8):
        payload_ref[device : device + 8] = payload_ref[0:8]
    if info is not None:
        lane = lax.broadcasted_iota(jnp.int32, (1, 128), 1)
        for device in range(N_DEV):
            payload_ref[device, :, pl.ds(STATE_LANES, 128)] = jnp.where(lane == 29, 1.0 * device, tail)


def pack_kernel(pair_ref, count_ref, position_ref, strength_ref, far_ref, row_ref, *out_refs):
    row_ref[...] = jnp.concatenate([far_ref[0:1], far_ref[1:2]], axis=1)
    zero = jnp.zeros((2, 2 * BS), jnp.float32)
    state = jnp.concatenate([position_ref[...], strength_ref[...], zero], axis=0)
    lane = lax.broadcasted_iota(jnp.int32, (1, 128), 1)
    info = jnp.zeros((1, 128), jnp.int32)
    for side in range(2):
        for slot in range(6):
            info = jnp.where(lane == 16 + 6 * side + slot, pair_ref[side, slot], info)
    info = jnp.where(lane == 28, count_ref[0], info)
    publish([state[:, 0:BS], state[:, BS:]], info.astype(jnp.float32), *out_refs)


def visit_counts(info):
    lane = lax.broadcasted_iota(jnp.int32, (N_DEV, 128), 1)
    first = lane < 22
    partner = jnp.where(first, pltpu.roll(info, 128 - 6, 1), pltpu.roll(info, 6, 1))
    slot = jnp.where(first, lane - 16, lane - 22).astype(jnp.float32)
    own = info - 2.0 * info[:, 29:30]
    live = (slot >= 0.0) & (slot < info[:, 28:29]) & (lane < 28) & (own >= 0.0) & (own < 2.0)
    codes = jnp.where(live, own * 64.0 + partner, -1.0).T
    code = lax.broadcasted_iota(jnp.int32, (128, N_DEV), 0).astype(jnp.float32)
    times = jnp.zeros((128, N_DEV), jnp.float32)
    for row in range(16, 28):
        times = times + jnp.where(code == codes[row : row + 1], 1.0, 0.0)
    counts = lax.dot_general(
        jnp.ones((8, N_DEV), jnp.float32),
        times,
        (((1,), (1,)), ((), ())),
        preferred_element_type=jnp.float32,
    )
    return counts.astype(jnp.int32)


def moment_kernel(region_ref, moment_ref):
    columns = region_ref[:, 0, STATE_LANES:].T
    rows = [columns[8 * t + c : 8 * t + c + 1] for c in range(6) for t in range(2)]
    table = jnp.concatenate(rows, axis=1)
    for group in range(N_GROUP):
        moment_ref[group] = table


def self_kernel(mine_ref, *refs):
    if len(refs) == 2:
        out_ref, mats = refs
    else:
        region_ref, out_ref, count_ref, mats = refs
        tails = region_ref[:, 0, STATE_LANES:]
        count_ref[...] = visit_counts(tails)
    for block in range(2):
        state = mine_ref[block]
        centre = centre_of(state)
        target = state - centre
        fill_kernels(target, target.T, mats.at[block], BS)
        out_ref[block, 0:16] = weighted_sums(target, mats.at[block], BS)
        out_ref[block, 16:24] = target
        out_ref[block, 24:32] = centre


def visit_list(count_ref, list_ref):
    def add(code, place):
        times = count_ref[0, code]
        list_ref[place] = times * 128 + code
        return place + jnp.where(times > 0, 1, 0)

    place = lax.fori_loop(0, 128, add, jnp.int32(1), unroll=16)
    list_ref[0] = place - 1


def near_kernel(count_ref, self_ref, region_ref, sum_ref, mats, list_ref, count_smem, sem):
    copy = pltpu.make_async_copy(count_ref, count_smem, sem)
    copy.start()
    copy.wait()
    visit_list(count_smem, list_ref)
    sum_ref[...] = self_ref[:, 0:16]

    def visit(place, slot):
        code = list_ref[place]
        times = (code >> 7).astype(jnp.float32)
        block = (code >> 6) & 1
        source = code & 63
        rows = []
        for c in range(6):
            lanes = pl.ds(pl.multiple_of(2 * BS * c + BS * (source & 1), BS), BS)
            rows.append(region_ref[source >> 1, :, lanes])
        rows.append(jnp.zeros((2, BS), jnp.float32))
        rows = jnp.concatenate(rows, axis=0) - self_ref[block, 24:32]
        fill_kernels(self_ref[block, 16:24], rows.T, mats.at[slot], BS)
        return block, times * weighted_sums(rows, mats.at[slot], BS)

    def visit_two(index, carry):
        block_a, sums_a = visit(2 * index + 1, 0)
        block_b, sums_b = visit(2 * index + 2, 1)
        sum_ref[block_a] += sums_a
        sum_ref[block_b] += sums_b
        return carry

    count = list_ref[0]
    lax.fori_loop(0, count >> 1, visit_two, 0)

    @pl.when(count & 1 == 1)
    def _():
        block, sums = visit(count, 0)
        sum_ref[block] += sums


def far_sources(far_ref, moment_ref):
    table = moment_ref[:, 0, :]
    table = jnp.concatenate(
        [table[:, REGION_BLOCKS * c : REGION_BLOCKS * c + REGION_BLOCKS] for c in range(6)], axis=0
    )
    size = table.shape[0]
    high = table.astype(jnp.bfloat16).astype(jnp.float32)
    middle = (table - high).astype(jnp.bfloat16).astype(jnp.float32)
    parts = jnp.concatenate([high, middle, table - high - middle], axis=0).astype(jnp.bfloat16)
    wanted = far_ref[...]
    place = (wanted & 1) * N_DEV + ((wanted >> 1) & (N_DEV - 1))
    lanes = lax.broadcasted_iota(jnp.int32, (REGION_BLOCKS, 128), 0)
    chosen = jnp.where(lanes == place, 1.0, 0.0).astype(jnp.bfloat16)
    found = jnp.dot(parts, chosen, preferred_element_type=jnp.float32)
    found = found[0:size] + found[size : 2 * size] + found[2 * size :]
    groups = lax.broadcasted_iota(jnp.int32, (N_GROUP, 128), 0)
    mine = groups == wanted >> 6
    rows = []
    for c in range(6):
        part = found[N_GROUP * c : N_GROUP * c + N_GROUP]
        rows.append(jnp.sum(jnp.where(mine, part, 0.0), axis=0, keepdims=True))
    return jnp.concatenate(rows + [jnp.zeros((2, 128), jnp.float32)], axis=0)


def far_kernel(last, far_ref, mine_ref, self_ref, sum_ref, moment_ref, *refs):
    *outs, mats = refs
    centres = [self_ref[block, 24:32][:, 0:64] for block in range(2)]
    rows = far_sources(far_ref, moment_ref) - jnp.concatenate(centres, axis=1)
    columns = rows.T
    blocks = []
    for block in range(2):
        target = self_ref[block, 16:24]
        source = rows[:, 64 * block : 64 * block + 64]
        fill_kernels(target, columns[64 * block : 64 * block + 64], mats.at[block], 64)
        sums = sum_ref[block] + weighted_sums(source, mats.at[block], 64)
        new = mine_ref[block, 0:6] + advance_rows(target, sums)
        blocks.append(jnp.concatenate([new, jnp.zeros((2, BS), jnp.float32)], axis=0))
    if last:
        position_ref, strength_ref = outs
        state = jnp.concatenate(blocks, axis=1)
        position_ref[...] = state[0:3]
        strength_ref[...] = state[3:6]
    else:
        publish(blocks, None, *outs)


def f32(*shape):
    return jax.ShapeDtypeStruct(shape, jnp.float32)


def kept(*shape):
    return pltpu.VMEM(shape, jnp.float32)


def keep(value):
    return pltpu.with_memory_space_constraint(value, VMEM)


def in_vmem(count):
    return [pl.BlockSpec(memory_space=VMEM)] * count


def in_smem(count):
    return [pl.BlockSpec(memory_space=SMEM)] * count


PUBLISHED = (kept(N_DEV, 1, WIDTH), kept(2, 8, BS))


def pack(pair_list, pair_count, positions, strengths, far_list):
    return pl.pallas_call(
        pack_kernel,
        out_shape=(pltpu.VMEM((1, 128), jnp.int32),) + PUBLISHED,
        in_specs=in_smem(2) + in_vmem(3),
        out_specs=tuple(in_vmem(3)),
        name="pack",
    )(pair_list, pair_count, positions, strengths, far_list.T)


def moments_of(region):
    return pl.pallas_call(
        moment_kernel,
        out_shape=kept(N_GROUP, 1, 6 * REGION_BLOCKS),
        in_specs=in_vmem(1),
        out_specs=in_vmem(1)[0],
        name="moments",
    )(region)


def self_terms(mine, *pair_operands):
    out_shape, out_specs, in_specs = (kept(2, 32, BS),), in_vmem(1), in_vmem(1)
    if pair_operands:
        out_shape += (pltpu.VMEM((8, 128), jnp.int32),)
        out_specs = in_vmem(2)
        in_specs = in_vmem(2)
    return pl.pallas_call(
        self_kernel,
        out_shape=out_shape,
        in_specs=in_specs,
        out_specs=tuple(out_specs),
        scratch_shapes=[pltpu.VMEM((2, 4, BS, BS), jnp.bfloat16)],
        cost_estimate=pl.CostEstimate(flops=4000000, bytes_accessed=60000, transcendentals=130000),
        name="self_terms",
    )(keep(mine), *pair_operands)


def near(counts, own, region):
    return pl.pallas_call(
        near_kernel,
        out_shape=kept(2, 16, BS),
        in_specs=in_vmem(3),
        out_specs=in_vmem(1)[0],
        scratch_shapes=[
            pltpu.VMEM((2, 4, BS, BS), jnp.bfloat16),
            pltpu.SMEM((136,), jnp.int32),
            pltpu.SMEM((8, 128), jnp.int32),
            pltpu.SemaphoreType.DMA(()),
        ],
        cost_estimate=pl.CostEstimate(flops=20000000, bytes_accessed=600000, transcendentals=500000),
        name="near",
    )(keep(counts), keep(own), region)


def far(far_row, mine, own, sums, moments, last):
    out_shape = (f32(3, 2 * BS), f32(3, 2 * BS)) if last else PUBLISHED
    return pl.pallas_call(
        functools.partial(far_kernel, last),
        out_shape=out_shape,
        in_specs=in_vmem(5),
        out_specs=tuple(in_vmem(len(out_shape))),
        scratch_shapes=[pltpu.VMEM((2, 4, 64, BS), jnp.bfloat16)],
        name="far",
    )(keep(far_row), keep(mine), keep(own), keep(sums), keep(moments))


def exchange(value, axis):
    return lax.all_to_all(value, axis, 0, 0, tiled=True)


def body(positions, strengths, pair_list, pair_count, far_list):
    far_row, payload, mine = pack(pair_list, pair_count, positions, strengths, far_list)
    counts = None
    for step in range(STEPS):
        first, last = step == 0, step == STEPS - 1
        region = keep(exchange(payload, "dev"))
        moments = exchange(moments_of(region), "group")
        if first:
            own, counts = self_terms(mine, region)
        else:
            (own,) = self_terms(mine)
        sums = near(counts, own, region)
        result = far(far_row, mine, own, sums, moments, last)
        if not last:
            payload, mine = result
    return result


def solution(mesh):
    split = P(None, ("group", "dev"))
    return jax.shard_map(
        body,
        mesh=mesh,
        in_specs=(split, split, split, P(("group", "dev")), split),
        out_specs=(split, split),
        check_vma=False,
    )
```
